128 devices in a mesh: blk: 8 (over y, core), sub: 16 (over x, z).
Axes of the slice: x: 4, y: 4, z: 4, core: 2. Of those that a mesh axis runs over, the one named last changes fastest.
Arguments:
- points: bfloat16 [131072, 384], P(('blk', 'sub')), may hold values from -6 to 6
- hilbert_pos: int32 [131072], P(('blk', 'sub')), may hold values from 0 to 131071, as said below
- segment_ids: int32 [131072], P(('blk', 'sub')), may hold values from 0 to 255, never falling along the last dimension, each value on 1 to 1024 neighbouring positions
- cotangent: bfloat16 [131072, 384], P(('blk', 'sub')), may hold values from -6 to 6
- w_qkv: bfloat16 [384, 1152], replicated, may hold values from -3 to 3
- w_proj: bfloat16 [384, 384], replicated, may hold values from -0.3125 to 0.3125
- w_fc1: bfloat16 [384, 1536], replicated, may hold values from -0.3125 to 0.3125
- w_fc2: bfloat16 [1536, 384], replicated, may hold values from -0.15625 to 0.15625
Outputs:
- output: bfloat16 [131072, 384], P(('blk', 'sub'))
- grad_points: bfloat16 [131072, 384], P(('blk', 'sub'))
- grad_qkv: float32 [384, 1152], replicated
- grad_proj: float32 [384, 384], replicated
- grad_fc1: float32 [384, 1536], replicated
- grad_fc2: float32 [1536, 384], replicated
The draws below stay inside these ranges and needn't reach their ends.
Inputs may be any that keep to these rules, and one draw needn't show every extreme that they name: hilbert_pos is a permutation of all positions; the 1024 points of one device land on the blocks of 1024 Hilbert positions of at most 64 devices, consecutive in device order with wrap-around; at most 32 of them on any one device's block, and 32 is reached in every draw.
All inputs are finite; a program needn't handle non-finite values.
Results may differ from the reference program's by a relative error of at most 0.02.
The reference program's roundings to bfloat16 on the way (of `normed`, `packed`, `weights`, `attended`, `middle`, `normed_again` and `hidden`) count: a program that leaves them out, or rounds other values in their place, can miss the bound.
Values may be sent and summed in bfloat16 or wider, within the bound.
No kernel may reach another device: no remote copies, remote signals or barrier semaphores. Data moves between devices by JAX's collectives and lax.ppermute only.
A program may use at most 128 MiB of HBM per device.

```python
import math
import jax
import jax.numpy as jnp
import numpy as np
from jax import lax

D = 384
HEADS = 12
FF = 1536
PATCH = 1024
P_DEV = 1024
SHARDS = 128
CAP = 32
POINTS = 131072


def draw_hilbert_pos(key, part):
    key = jax.random.fold_in(key, 11)
    key_count, key_dest, key_source, key_order = jax.random.split(key, 4)
    reach = SHARDS // 2
    half = CAP // 2
    offsets = jax.random.randint(key_count, (reach // 2,), -half, half + 1)
    offsets = offsets.at[0].set(half)
    profile = jnp.stack([half + offsets, half - offsets], axis=1).reshape(reach)
    profile = jnp.concatenate([profile, jnp.zeros((SHARDS - reach,), jnp.int32)])
    start_block = jax.random.permutation(key_order, SHARDS)
    target = jnp.arange(SHARDS)[None, :]
    counts = profile[(target - start_block[:, None]) % SHARDS]
    before_source = jnp.cumsum(counts, axis=0) - counts
    running = jnp.cumsum(counts, axis=1)
    first = running - counts
    within = jnp.arange(P_DEV)
    dest = jax.vmap(lambda limits: jnp.searchsorted(limits, within, side='right'))(running).astype(jnp.int32)
    row_index = jnp.arange(SHARDS)[:, None]
    local = before_source[row_index, dest] + within[None, :] - first[row_index, dest]
    shuffle_dest = jax.vmap(lambda sub_key: jax.random.permutation(sub_key, P_DEV))(jax.random.split(key_dest, SHARDS))
    position = dest * P_DEV + shuffle_dest[dest, local]
    shuffle_source = jax.vmap(lambda sub_key: jax.random.permutation(sub_key, P_DEV))(jax.random.split(key_source, SHARDS))
    position = jnp.take_along_axis(position, shuffle_source, axis=1)
    return position.reshape(POINTS).astype(jnp.int32)


def draw_w_qkv(key, part):
    key = jax.random.fold_in(key, 5)
    key_base = jax.random.fold_in(key, 0)
    base = jax.random.normal(key_base, (D, 3 * D), jnp.float32) / jnp.sqrt(jnp.float32(D))
    queries = base[:, :D]
    keys = base[:, D:2 * D]
    values = base[:, 2 * D:]
    return jnp.clip(jnp.concatenate([queries, keys, values], axis=1), -3.0, 3.0).astype(jnp.bfloat16)


def levels(own_key, dims, pieces, low, largest):
    def one(axis_at, parts):
        heights = jax.random.uniform(jax.random.fold_in(jax.random.fold_in(own_key, 6), axis_at), (parts,), jnp.float32, low / len(pieces), largest / len(pieces))
        return jnp.repeat(jnp.exp(heights), dims[axis_at] // parts).reshape((-1,) + (1,) * (len(dims) - axis_at - 1))

    gain = one(*pieces[0])
    for cut in pieces[1:]:
        gain = gain * one(*cut)
    return gain


def split_up(count, total, limit, skew):
    weights = [(1 << 20) // math.isqrt(rank ** skew) + 1 for rank in range(2, count + 1)]
    spare, given = total - limit - (count - 1), [1] * (count - 1)
    while spare > 0:
        candidates = [i for i in range(count - 1) if given[i] < limit]
        pool, remaining = sum([weights[i] for i in candidates]), spare
        for i in candidates:
            extra = min(limit - given[i], max(1, remaining * weights[i] // pool), spare)
            given[i] = given[i] + extra
            spare = spare - extra
    return np.array([limit] + given)


def uneven(own_key, count, total, limit, slope):
    if count == 2:
        one = jax.random.randint(own_key, (), max(1, total - limit), min(limit, total - 1) + 1)
        return jnp.stack([one, total - one])
    sizes = jnp.asarray(split_up(count, total, limit, slope), jnp.int32)
    pairs = (count - 1) // 2
    giver, sink = sizes[1:1 + 2 * pairs:2], sizes[2:2 + 2 * pairs:2]
    margin = jnp.minimum(giver - 1, limit - sink)
    moved = jax.random.randint(jax.random.fold_in(own_key, 1), (pairs,), 0, 1 << 20) % (margin + 1)
    sizes = sizes.at[1:1 + 2 * pairs:2].set(giver - moved).at[2:2 + 2 * pairs:2].set(sink + moved)
    return sizes[jax.random.permutation(jax.random.fold_in(own_key, 2), count)]


def normal_values(stream_key, extent, scale, most, shards=(), kind=jnp.bfloat16):
    gain = levels(stream_key, extent, shards, -0.22, 0.18) if shards else 1.0
    values = jax.random.normal(stream_key, extent, jnp.float32) * scale * gain
    return jnp.minimum(jnp.maximum(values, -most), most).astype(kind)


def setup_inputs(seed: int = 0) -> dict:
    key_list = jax.random.split(jax.random.key(seed), 9)
    return {
        "points": normal_values(key_list[0], (POINTS, D), 1.0, 6.0, ((0, 128),)),
        "hilbert_pos": draw_hilbert_pos(jax.random.fold_in(key_list[8], 71), 0),
        "segment_ids": jnp.searchsorted(jnp.cumsum(uneven(key_list[2], 2 * POINTS // PATCH, POINTS, PATCH, 2)), jnp.arange(POINTS), side="right").astype(jnp.int32),
        "cotangent": normal_values(key_list[3], (POINTS, D), 1.0, 6.0, ((0, 128),)),
        "w_qkv": draw_w_qkv(jax.random.fold_in(key_list[8], 71), 0),
        "w_proj": normal_values(key_list[5], (D, D), D ** -0.5, 0.3125),
        "w_fc1": normal_values(key_list[6], (D, FF), D ** -0.5, 0.3125),
        "w_fc2": normal_values(key_list[7], (FF, D), FF ** -0.5, 0.15625),
    }


EPSILON = 1e-05

def norm_rows(values):
    centred = values - lax.optimization_barrier(jnp.mean(values, axis=-1, keepdims=True))
    spread = lax.optimization_barrier(jnp.mean(centred * centred, axis=-1, keepdims=True))
    return centred * lax.rsqrt(spread + EPSILON)

def attend(packed, segments):
    length = packed.shape[0]
    features = packed.shape[1] // 3
    head_dim = features // HEADS
    split_heads = packed.reshape(length, 3, HEADS, head_dim).transpose(1, 2, 0, 3)
    allowed = segments[:, None] == segments[None, :]
    scaling = 1.0 / math.sqrt(head_dim)

    def one_head(triple):
        queries, keys, values = triple
        scores = jnp.dot(queries, keys.T, preferred_element_type=jnp.float32) * scaling
        scores = jnp.where(allowed, scores, -1e+30)
        shifted = jnp.exp(scores - lax.optimization_barrier(jnp.max(scores, axis=-1, keepdims=True)))
        weights = (shifted / lax.optimization_barrier(jnp.sum(shifted, axis=-1, keepdims=True))).astype(jnp.bfloat16)
        return jnp.dot(weights, values, preferred_element_type=jnp.float32).astype(jnp.bfloat16)
    mixed = lax.map(jax.checkpoint(one_head), (split_heads[0], split_heads[1], split_heads[2]))
    return mixed.transpose(1, 0, 2).reshape(length, features)

def attention_half(inputs, segments, w_qkv, w_proj):
    row_count, features = inputs.shape
    normed = norm_rows(inputs.astype(jnp.float32)).astype(jnp.bfloat16)
    packed = jnp.dot(normed, w_qkv, preferred_element_type=jnp.float32).astype(jnp.bfloat16)
    patches = row_count // PATCH
    attended = lax.map(lambda pair: attend(pair[0], pair[1]), (packed.reshape(patches, PATCH, 3 * features), segments.reshape(patches, PATCH)))
    attended = attended.reshape(row_count, features)
    return (inputs.astype(jnp.float32) + jnp.dot(attended, w_proj, preferred_element_type=jnp.float32)).astype(jnp.bfloat16)

def mlp_half(middle, w_fc1, w_fc2):
    normed_again = norm_rows(middle.astype(jnp.float32)).astype(jnp.bfloat16)
    hidden = jax.nn.gelu(jnp.dot(normed_again, w_fc1, preferred_element_type=jnp.float32), approximate=False).astype(jnp.bfloat16)
    return (middle.astype(jnp.float32) + jnp.dot(hidden, w_fc2, preferred_element_type=jnp.float32)).astype(jnp.bfloat16)

def reference(points, hilbert_pos, segment_ids, cotangent, w_qkv, w_proj, w_fc1, w_fc2):
    features = points.shape[1]
    ordered = jnp.zeros_like(points).at[hilbert_pos].set(points).reshape(SHARDS, P_DEV, features)
    ordered_grad = jnp.zeros_like(cotangent).at[hilbert_pos].set(cotangent).reshape(SHARDS, P_DEV, features)
    groups = segment_ids.reshape(SHARDS, P_DEV)

    def shard_step(totals, piece):
        inputs, segments, upstream = piece
        middle, pull_attention = jax.vjp(lambda values, first, second: attention_half(values, segments, first, second), inputs, w_qkv, w_proj)
        result, pull_mlp = jax.vjp(mlp_half, middle, w_fc1, w_fc2)
        grad_middle, grad_first, grad_second = pull_mlp(upstream)
        grad_inputs, grad_query, grad_output = pull_attention(grad_middle)
        grads = (grad_query, grad_output, grad_first, grad_second)
        totals = tuple((total + grad.astype(jnp.float32) for total, grad in zip(totals, grads)))
        return (totals, (result, grad_inputs))
    start = tuple((jnp.zeros(matrix.shape, jnp.float32) for matrix in (w_qkv, w_proj, w_fc1, w_fc2)))
    totals, (results, input_grads) = lax.scan(shard_step, start, (ordered, groups, ordered_grad))
    output = results.reshape(-1, features)[hilbert_pos]
    grad_points = input_grads.reshape(-1, features)[hilbert_pos]
    return (output, grad_points, totals[0], totals[1], totals[2], totals[3])
```

```python
import math

import jax
import jax.numpy as jnp
from jax import lax
from jax.experimental import pallas as pl
from jax.experimental.pallas import tpu as pltpu
from jax.sharding import PartitionSpec as P

AXES = ("blk", "sub")
ROWS = 1024
D = 384
FF = 1536
LANES = 128
HEAD_DIM = 32
GROUPS = D // LANES
HEADS_PER_GROUP = LANES // HEAD_DIM
SHARDS = 128
CAP = 32
SLOTS = SHARDS * CAP
STEP_SHARDS = 16
STEP_SLOTS = STEP_SHARDS * CAP
STEPS = SHARDS // STEP_SHARDS
WIRE_ROWS = 3 * CAP + 2
EPSILON = 1e-05
SCALING = 1.0 / math.sqrt(HEAD_DIM)
LOG2E = 1.4426950408889634
MASKED = -1e30
TILE = 256
BF = jnp.bfloat16
F32 = jnp.float32
VMEM_LIMIT = 56 * 1024 * 1024

NT = (((1,), (1,)), ((), ()))


def dot(a, b):
    return jnp.dot(a, b, preferred_element_type=F32)


def dot_nt(a, b):
    return lax.dot_general(a, b, NT, preferred_element_type=F32)


def iota(shape, axis):
    return lax.broadcasted_iota(jnp.int32, shape, axis)


def params(grid_dims=1):
    return pltpu.CompilerParams(
        vmem_limit_bytes=VMEM_LIMIT,
        dimension_semantics=("arbitrary",) * grid_dims,
    )


def cost(flops, bytes_accessed, transcendentals=0):
    return pl.CostEstimate(
        flops=int(flops), bytes_accessed=int(bytes_accessed), transcendentals=int(transcendentals)
    )


def row_to_column(row):
    return jnp.broadcast_to(row, (8, row.shape[1])).T[:, 0:1]


def one_hot_slots(slot_row, first):
    ids = iota((STEP_SLOTS, ROWS), 0) + first
    return (ids == slot_row).astype(F32).astype(BF)


def pack_points_kernel(lane_ref, pos_ref, x_ref, out_ref, slot_ref, high_s, low_s):
    step = pl.program_id(0)

    @pl.when(step == 0)
    def _():
        pos = pos_ref[...]
        target = pos >> 10
        offset = pos & (ROWS - 1)
        member = iota((SHARDS, ROWS), 0) == target
        member_bf = member.astype(F32).astype(BF)
        before = (iota((ROWS, ROWS), 0) < iota((ROWS, ROWS), 1)).astype(F32).astype(BF)
        earlier = dot(member_bf, before)
        rank = jnp.sum(jnp.where(member, earlier, 0.0), axis=0, keepdims=True).astype(jnp.int32)
        slot_ref[...] = target * CAP + rank
        lane = (iota((LANES, ROWS), 0) == rank + lane_ref[0]).astype(F32).astype(BF)
        high = ((offset >> 5) + 1).astype(F32)
        low = (offset & 31).astype(F32)
        high_s[...] = dot_nt(jnp.where(member, high, 0.0).astype(BF), lane)
        low_s[...] = dot_nt(jnp.where(member, low, 0.0).astype(BF), lane)

    picked = dot(one_hot_slots(slot_ref[...], step * STEP_SLOTS), x_ref[...]).astype(BF)
    for piece in range(3):
        out_ref[:, piece * CAP : (piece + 1) * CAP, :] = picked[
            :, piece * LANES : (piece + 1) * LANES
        ].reshape(STEP_SHARDS, CAP, LANES)
    first = pl.multiple_of(step * STEP_SHARDS, STEP_SHARDS)
    high = high_s[pl.ds(first, STEP_SHARDS), :]
    low = low_s[pl.ds(first, STEP_SHARDS), :]
    for s in range(STEP_SHARDS):
        pair = jnp.concatenate([high[s : s + 1], low[s : s + 1]], axis=0)
        out_ref[s, 3 * CAP : WIRE_ROWS, :] = pair.astype(BF)


def pack_points(first_lane, pos_row, points):
    return pl.pallas_call(
        pack_points_kernel,
        grid=(STEPS,),
        in_specs=[
            pl.BlockSpec(memory_space=pltpu.SMEM),
            pl.BlockSpec((1, ROWS), lambda i: (0, 0)),
            pl.BlockSpec((ROWS, D), lambda i: (0, 0)),
        ],
        out_specs=[
            pl.BlockSpec((STEP_SHARDS, WIRE_ROWS, LANES), lambda i: (i, 0, 0)),
            pl.BlockSpec((1, ROWS), lambda i: (0, 0)),
        ],
        out_shape=[
            jax.ShapeDtypeStruct((SHARDS, WIRE_ROWS, LANES), BF),
            jax.ShapeDtypeStruct((1, ROWS), jnp.int32),
        ],
        scratch_shapes=[pltpu.VMEM((SHARDS, LANES), F32), pltpu.VMEM((SHARDS, LANES), F32)],
        compiler_params=params(),
        cost_estimate=cost(2 * SLOTS * ROWS * D, 8 * SLOTS * D),
        name="pack_points",
    )(first_lane, pos_row, points)


def pack_rows_kernel(slot_ref, x_ref, out_ref):
    picked = dot(one_hot_slots(slot_ref[...], pl.program_id(0) * STEP_SLOTS), x_ref[...])
    out_ref[...] = picked.astype(BF).reshape(STEP_SHARDS, CAP, D)


def pack_rows(slot_row, values):
    return pl.pallas_call(
        pack_rows_kernel,
        grid=(STEPS,),
        in_specs=[
            pl.BlockSpec((1, ROWS), lambda i: (0, 0)),
            pl.BlockSpec((ROWS, D), lambda i: (0, 0)),
        ],
        out_specs=pl.BlockSpec((STEP_SHARDS, CAP, D), lambda i: (i, 0, 0)),
        out_shape=jax.ShapeDtypeStruct((SHARDS, CAP, D), BF),
        compiler_params=params(),
        cost_estimate=cost(2 * SLOTS * ROWS * D, 4 * SLOTS * D),
        name="pack_rows",
    )(slot_row, values)


def unpack_rows_kernel(slot_ref, home_ref, out_ref, column_s, total_s):
    step = pl.program_id(0)

    @pl.when(step == 0)
    def _():
        column_s[...] = jnp.broadcast_to(
            row_to_column(slot_ref[...].astype(F32)).astype(jnp.int32), (ROWS, LANES)
        )
        total_s[...] = jnp.zeros_like(total_s)

    wide = jnp.concatenate([column_s[...]] * (STEP_SLOTS // LANES), axis=1)
    hot = (iota((ROWS, STEP_SLOTS), 1) + step * STEP_SLOTS == wide).astype(F32).astype(BF)
    total_s[...] += dot(hot, home_ref[...].reshape(STEP_SLOTS, D))

    @pl.when(step == STEPS - 1)
    def _():
        out_ref[...] = total_s[...].astype(BF)


def unpack_rows(slot_row, home):
    return pl.pallas_call(
        unpack_rows_kernel,
        grid=(STEPS,),
        in_specs=[
            pl.BlockSpec((1, ROWS), lambda i: (0, 0)),
            pl.BlockSpec((STEP_SHARDS, CAP, D), lambda i: (i, 0, 0)),
        ],
        out_specs=pl.BlockSpec((ROWS, D), lambda i: (0, 0)),
        out_shape=jax.ShapeDtypeStruct((ROWS, D), BF),
        scratch_shapes=[pltpu.VMEM((ROWS, LANES), jnp.int32), pltpu.VMEM((ROWS, D), F32)],
        compiler_params=params(),
        cost_estimate=cost(2 * SLOTS * ROWS * D, 4 * SLOTS * D),
        name="unpack_rows",
    )(slot_row, home)


def norm_parts(values):
    centred = values - jnp.mean(values, axis=-1, keepdims=True)
    spread = jnp.mean(centred * centred, axis=-1, keepdims=True)
    scale = lax.rsqrt(spread + EPSILON)
    return centred * scale, scale


def norm_pull(normed, scale, upstream):
    across = jnp.mean(upstream, axis=-1, keepdims=True)
    along = jnp.mean(upstream * normed, axis=-1, keepdims=True)
    return scale * (upstream - across - normed * along)


def landing_one_hot(landing):
    return (iota((ROWS, STEP_SLOTS), 0) == landing).astype(F32).astype(BF)


def land_points_kernel(recv_ref, w_ref, ordered_ref, packed_ref, landing_ref, total_s):
    step = pl.program_id(0)

    @pl.when(step == 0)
    def _():
        total_s[...] = jnp.zeros_like(total_s)

    pieces = []
    for group in range(STEP_SHARDS // 4):
        pair = recv_ref[4 * group, 3 * CAP : WIRE_ROWS, :].astype(F32)
        for other in range(1, 4):
            pair = pair + recv_ref[4 * group + other, 3 * CAP : WIRE_ROWS, :].astype(F32)
        pieces.append((pair[0:1] - 1.0) * 32.0 + pair[1:2])
    landing = jnp.concatenate(pieces, axis=1).astype(jnp.int32)
    landing_ref[0] = landing
    rows = jnp.concatenate(
        [
            recv_ref[:, piece * CAP : (piece + 1) * CAP, :].reshape(STEP_SLOTS, LANES)
            for piece in range(3)
        ],
        axis=1,
    )
    total_s[...] += dot(landing_one_hot(landing), rows)

    @pl.when(step == STEPS - 1)
    def _():
        ordered = total_s[...]
        ordered_ref[...] = ordered.astype(BF)
        normed, _ = norm_parts(ordered)
        packed_ref[...] = dot(normed.astype(BF), w_ref[...]).astype(BF)


def land_points(received, w_qkv):
    return pl.pallas_call(
        land_points_kernel,
        grid=(STEPS,),
        in_specs=[
            pl.BlockSpec((STEP_SHARDS, WIRE_ROWS, LANES), lambda i: (i, 0, 0)),
            pl.BlockSpec((D, 3 * D), lambda i: (0, 0)),
        ],
        out_specs=[
            pl.BlockSpec((ROWS, D), lambda i: (0, 0)),
            pl.BlockSpec((ROWS, 3 * D), lambda i: (0, 0)),
            pl.BlockSpec((1, 1, STEP_SLOTS), lambda i: (i, 0, 0)),
        ],
        out_shape=[
            jax.ShapeDtypeStruct((ROWS, D), BF),
            jax.ShapeDtypeStruct((ROWS, 3 * D), BF),
            jax.ShapeDtypeStruct((STEPS, 1, STEP_SLOTS), jnp.int32),
        ],
        scratch_shapes=[pltpu.VMEM((ROWS, D), F32)],
        compiler_params=params(),
        cost_estimate=cost(2 * SLOTS * ROWS * D + 6 * ROWS * D * D, 6 * SLOTS * D),
        name="land_points",
    )(received, w_qkv)


def land_rows_kernel(landing_ref, recv_ref, out_ref, total_s):
    step = pl.program_id(0)

    @pl.when(step == 0)
    def _():
        total_s[...] = jnp.zeros_like(total_s)

    total_s[...] += dot(landing_one_hot(landing_ref[0]), recv_ref[...].reshape(STEP_SLOTS, D))

    @pl.when(step == STEPS - 1)
    def _():
        out_ref[...] = total_s[...].astype(BF)


def land_rows(landing, received):
    return pl.pallas_call(
        land_rows_kernel,
        grid=(STEPS,),
        in_specs=[
            pl.BlockSpec((1, 1, STEP_SLOTS), lambda i: (i, 0, 0)),
            pl.BlockSpec((STEP_SHARDS, CAP, D), lambda i: (i, 0, 0)),
        ],
        out_specs=pl.BlockSpec((ROWS, D), lambda i: (0, 0)),
        out_shape=jax.ShapeDtypeStruct((ROWS, D), BF),
        scratch_shapes=[pltpu.VMEM((ROWS, D), F32)],
        compiler_params=params(),
        cost_estimate=cost(2 * SLOTS * ROWS * D, 4 * SLOTS * D),
        name="land_rows",
    )(landing, received)


def return_one_hot(landing):
    column = row_to_column(landing.astype(F32)).astype(jnp.int32)
    return (iota((STEP_SLOTS, ROWS), 1) == column).astype(F32).astype(BF)


def return_rows_kernel(landing_ref, x_ref, out_ref):
    picked = dot(return_one_hot(landing_ref[0]), x_ref[...])
    out_ref[...] = picked.astype(BF).reshape(STEP_SHARDS, CAP, D)


def return_rows(landing, values):
    return pl.pallas_call(
        return_rows_kernel,
        grid=(STEPS,),
        in_specs=[
            pl.BlockSpec((1, 1, STEP_SLOTS), lambda i: (i, 0, 0)),
            pl.BlockSpec((ROWS, D), lambda i: (0, 0)),
        ],
        out_specs=pl.BlockSpec((STEP_SHARDS, CAP, D), lambda i: (i, 0, 0)),
        out_shape=jax.ShapeDtypeStruct((SHARDS, CAP, D), BF),
        compiler_params=params(),
        cost_estimate=cost(2 * SLOTS * ROWS * D, 4 * SLOTS * D),
        name="return_rows",
    )(landing, values)


def three_parts(values):
    high = values.astype(BF)
    rest = values - high.astype(F32)
    middle = rest.astype(BF)
    return high, middle, (rest - middle.astype(F32)).astype(BF)


def write_bias(bias_s, column_ref, row_ref):
    bias_s[...] = jnp.where(column_ref[...] == row_ref[...], 0.0, MASKED)


def head_of_lane():
    return iota((ROWS, LANES), 1) // HEAD_DIM


def roll_lanes(values, by):
    return pltpu.roll(values.astype(F32), by % LANES, 1)


def query_side(q, head, owner, shift=None):
    near, far = (head + 1) % HEADS_PER_GROUP, (head + 2) % HEADS_PER_GROUP
    high, middle, low = (part.astype(F32) for part in three_parts(q * (SCALING * LOG2E)))
    first = jnp.where(owner == head, high, 0.0)
    second = jnp.where(
        owner == near,
        roll_lanes(middle, HEAD_DIM),
        jnp.where(owner == far, roll_lanes(low, 2 * HEAD_DIM), 0.0),
    )
    if shift is not None:
        lane = iota((ROWS, LANES), 1) - head * HEAD_DIM
        parts = [part.astype(F32) for part in three_parts(-shift)]
        for at, part in enumerate(parts):
            second = jnp.where(lane == at, part, second)
    return jnp.concatenate([first.astype(BF), second.astype(BF)], axis=1)


def key_side(k, head, owner, shifted):
    near, far = (head + 1) % HEADS_PER_GROUP, (head + 2) % HEADS_PER_GROUP
    second = jnp.where(
        owner == near,
        roll_lanes(k, HEAD_DIM),
        jnp.where(owner == far, roll_lanes(k, 2 * HEAD_DIM), 0.0),
    )
    if shifted:
        lane = iota((ROWS, LANES), 1) - head * HEAD_DIM
        second = jnp.where((lane >= 0) & (lane < 3), 1.0, second)
    return jnp.concatenate([k.astype(BF), second.astype(BF)], axis=1)


def attend_kernel(column_ref, row_ref, q_ref, k_ref, v_ref, mixed_ref, exact_ref, level_ref, bias_s):
    @pl.when(pl.program_id(0) == 0)
    def _():
        write_bias(bias_s, column_ref, row_ref)

    owner = head_of_lane()
    q, k, v = (ref[...].astype(F32) for ref in (q_ref, k_ref, v_ref))
    owner_tile = owner[:TILE]
    for head in range(HEADS_PER_GROUP):
        queries = query_side(q, head, owner)
        keys = key_side(k, head, owner, False)
        values = jnp.concatenate(
            [jnp.where(owner == head, v, 0.0).astype(BF), jnp.ones((ROWS, LANES), BF)], axis=1
        )
        for tile in range(ROWS // TILE):
            rows = slice(tile * TILE, (tile + 1) * TILE)
            scores = dot_nt(queries[rows], keys) + bias_s[rows, :]
            most = jnp.max(scores, axis=-1, keepdims=True)
            raised = jnp.exp2(scores - most).astype(BF)
            both = dot(raised, values)
            total = both[:, LANES:]
            result = both[:, :LANES] / total
            level = most + jnp.log2(total)
            if head == 0:
                exact_ref[rows, :] = result
                level_ref[rows, :] = level
            else:
                mine = owner_tile == head
                exact_ref[rows, :] = jnp.where(mine, result, exact_ref[rows, :])
                level_ref[rows, :] = jnp.where(mine, level, level_ref[rows, :])
    mixed_ref[...] = exact_ref[...].astype(BF)


def group_spec(first=0):
    return pl.BlockSpec((ROWS, LANES), lambda g: (0, first + g))


def whole(shape):
    return pl.BlockSpec(shape, lambda g: (0,) * len(shape))


def attend(segment_column, segment_row, packed):
    return pl.pallas_call(
        attend_kernel,
        grid=(GROUPS,),
        in_specs=[
            whole((ROWS, 1)),
            whole((1, ROWS)),
            group_spec(0),
            group_spec(GROUPS),
            group_spec(2 * GROUPS),
        ],
        out_specs=[group_spec()] * 3,
        out_shape=[
            jax.ShapeDtypeStruct((ROWS, D), BF),
            jax.ShapeDtypeStruct((ROWS, D), F32),
            jax.ShapeDtypeStruct((ROWS, D), F32),
        ],
        scratch_shapes=[pltpu.VMEM((ROWS, ROWS), F32)],
        compiler_params=params(),
        cost_estimate=cost(24e9, 8 * ROWS * D, 12 * ROWS * ROWS),
        name="attend",
    )(segment_column, segment_row, packed, packed, packed)


def attend_back_kernel(
    column_ref,
    row_ref,
    q_ref,
    k_ref,
    v_ref,
    up_ref,
    exact_ref,
    level_ref,
    dq_ref,
    dk_ref,
    dv_ref,
    bias_s,
    dqt_s,
    dk_s,
    dv_s,
):
    @pl.when(pl.program_id(0) == 0)
    def _():
        write_bias(bias_s, column_ref, row_ref)

    owner = head_of_lane()
    q, k, v, up = (ref[...].astype(F32) for ref in (q_ref, k_ref, v_ref, up_ref))
    level = level_ref[...]
    keys_t = k.T.astype(BF)
    from_head = iota((LANES, LANES), 0) // HEAD_DIM
    to_head = iota((LANES, LANES), 1) // HEAD_DIM
    spread = ((from_head + 1) % HEADS_PER_GROUP == to_head).astype(F32).astype(BF)
    delta = sum(dot(part, spread) for part in three_parts(up * exact_ref[...]))
    delta_parts = [part.astype(F32) for part in three_parts(-delta)]
    for head in range(HEADS_PER_GROUP):
        mine = owner == head
        near = (head + 1) % HEADS_PER_GROUP
        lane = iota((ROWS, LANES), 1) - near * HEAD_DIM
        queries = query_side(q, head, owner, level)
        keys = key_side(k, head, owner, True)
        up_mine = jnp.where(mine, up, 0.0)
        up_side = up_mine
        for at, part in enumerate(delta_parts):
            up_side = jnp.where(lane == at, part, up_side)
        up_side = up_side.astype(BF)
        up_mine = up_mine.astype(BF)
        value_side = jnp.where((lane >= 0) & (lane < 3), 1.0, v).astype(BF)
        query_mine = jnp.where(mine, q, 0.0).astype(BF)
        head_rows = slice(head * HEAD_DIM, (head + 1) * HEAD_DIM)
        for tile in range(ROWS // TILE):
            rows = slice(tile * TILE, (tile + 1) * TILE)
            weights = jnp.exp2(dot_nt(keys[rows], queries) + bias_s[rows, :])
            pulled = weights * dot_nt(value_side[rows], up_side)
            pulled = pulled.astype(BF)
            dv_part = dot(weights.astype(BF), up_mine)
            dk_part = dot(pulled, query_mine)
            dq_part = dot(keys_t[head_rows, rows], pulled)
            if head == 0:
                dv_s[rows, :] = dv_part
                dk_s[rows, :] = dk_part
            else:
                dv_s[rows, :] += dv_part
                dk_s[rows, :] += dk_part
            if tile == 0:
                dqt_s[head_rows, :] = dq_part
            else:
                dqt_s[head_rows, :] += dq_part
    dq_ref[...] = (dqt_s[...] * SCALING).T.astype(BF)
    dk_ref[...] = (dk_s[...] * SCALING).astype(BF)
    dv_ref[...] = dv_s[...].astype(BF)


def attend_back(segment_column, segment_row, packed, upstream, exact, level):
    return pl.pallas_call(
        attend_back_kernel,
        grid=(GROUPS,),
        in_specs=[
            whole((ROWS, 1)),
            whole((1, ROWS)),
            group_spec(0),
            group_spec(GROUPS),
            group_spec(2 * GROUPS),
            group_spec(),
            group_spec(),
            group_spec(),
        ],
        out_specs=[group_spec()] * 3,
        out_shape=[jax.ShapeDtypeStruct((ROWS, D), BF)] * 3,
        scratch_shapes=[
            pltpu.VMEM((ROWS, ROWS), F32),
            pltpu.VMEM((LANES, ROWS), F32),
            pltpu.VMEM((ROWS, LANES), F32),
            pltpu.VMEM((ROWS, LANES), F32),
        ],
        compiler_params=params(),
        cost_estimate=cost(60e9, 16 * ROWS * D, 12 * ROWS * ROWS),
        name="attend_back",
    )(segment_column, segment_row, packed, packed, packed, upstream, exact, level)


FF_STEP = 512
FF_STEPS = FF // FF_STEP


def mlp_kernel(
    ordered_ref,
    mixed_ref,
    up_ref,
    w_proj_ref,
    w1_ref,
    w2_ref,
    block_ref,
    d_middle_ref,
    d_mixed_ref,
    d_proj_ref,
    d_w1_ref,
    d_w2_ref,
    middle_s,
    normed_s,
    normed_t_s,
    up_t_s,
    out_s,
    d_normed_s,
):
    step = pl.program_id(0)
    up = up_ref[...]

    @pl.when(step == 0)
    def _():
        middle = (
            ordered_ref[...].astype(F32) + dot(mixed_ref[...], w_proj_ref[...])
        ).astype(BF)
        middle_s[...] = middle
        normed, _ = norm_parts(middle.astype(F32))
        normed = normed.astype(BF)
        normed_s[...] = normed
        normed_t_s[...] = normed.astype(F32).T.astype(BF)
        up_t_s[...] = up.astype(F32).T.astype(BF)
        out_s[...] = jnp.zeros_like(out_s)
        d_normed_s[...] = jnp.zeros_like(d_normed_s)

    w1, w2 = w1_ref[...], w2_ref[...]
    before = dot(normed_s[...], w1)
    d_hidden = dot_nt(up, w2).astype(BF).astype(F32)
    half = 0.5 * (1.0 + lax.erf(before * math.sqrt(0.5)))
    density = jnp.exp(before * before * -0.5) * (1.0 / math.sqrt(2.0 * math.pi))
    hidden = (before * half).astype(BF)
    d_before = (d_hidden * (half + before * density)).astype(BF)
    out_s[...] += dot(hidden, w2)
    d_w2_ref[...] = dot(up_t_s[...], hidden).T.astype(BF)
    d_w1_ref[...] = dot(normed_t_s[...], d_before).astype(BF)
    d_normed_s[...] += dot_nt(d_before, w1)

    @pl.when(step == FF_STEPS - 1)
    def _():
        middle = middle_s[...].astype(F32)
        block_ref[...] = (middle + out_s[...]).astype(BF)
        normed, scale = norm_parts(middle)
        pulled = norm_pull(normed, scale, d_normed_s[...].astype(BF).astype(F32)).astype(BF)
        d_middle = (up.astype(F32) + pulled.astype(F32)).astype(BF)
        d_middle_ref[...] = d_middle
        d_mixed_ref[...] = dot_nt(d_middle, w_proj_ref[...]).astype(BF)
        d_proj_ref[...] = dot(mixed_ref[...].astype(F32).T.astype(BF), d_middle).astype(BF)


def mlp(ordered, mixed, upstream, w_proj, w_fc1, w_fc2):
    rows = whole((ROWS, D))
    return pl.pallas_call(
        mlp_kernel,
        grid=(FF_STEPS,),
        in_specs=[
            rows,
            rows,
            rows,
            whole((D, D)),
            pl.BlockSpec((D, FF_STEP), lambda i: (0, i)),
            pl.BlockSpec((FF_STEP, D), lambda i: (i, 0)),
        ],
        out_specs=[
            rows,
            rows,
            rows,
            whole((D, D)),
            pl.BlockSpec((D, FF_STEP), lambda i: (0, i)),
            pl.BlockSpec((FF_STEP, D), lambda i: (i, 0)),
        ],
        out_shape=[
            jax.ShapeDtypeStruct((ROWS, D), BF),
            jax.ShapeDtypeStruct((ROWS, D), BF),
            jax.ShapeDtypeStruct((ROWS, D), BF),
            jax.ShapeDtypeStruct((D, D), BF),
            jax.ShapeDtypeStruct((D, FF), BF),
            jax.ShapeDtypeStruct((FF, D), BF),
        ],
        scratch_shapes=[
            pltpu.VMEM((ROWS, D), BF),
            pltpu.VMEM((ROWS, D), BF),
            pltpu.VMEM((D, ROWS), BF),
            pltpu.VMEM((D, ROWS), BF),
            pltpu.VMEM((ROWS, D), F32),
            pltpu.VMEM((ROWS, D), F32),
        ],
        compiler_params=params(),
        cost_estimate=cost(12 * ROWS * D * FF, 20 * ROWS * D, 2 * ROWS * FF),
        name="mlp",
    )(ordered, mixed, upstream, w_proj, w_fc1, w_fc2)


def inputs_back_kernel(ordered_ref, dq_ref, dk_ref, dv_ref, d_middle_ref, w_ref, out_ref):
    normed, scale = norm_parts(ordered_ref[...].astype(F32))
    d_normed = (
        dot_nt(dq_ref[...], w_ref[:, :D])
        + dot_nt(dk_ref[...], w_ref[:, D : 2 * D])
        + dot_nt(dv_ref[...], w_ref[:, 2 * D :])
    )
    pulled = norm_pull(normed, scale, d_normed.astype(BF).astype(F32)).astype(BF)
    out_ref[...] = (d_middle_ref[...].astype(F32) + pulled.astype(F32)).astype(BF)


def inputs_back(ordered, dq, dk, dv, d_middle, w_qkv):
    rows = whole((ROWS, D))
    return pl.pallas_call(
        inputs_back_kernel,
        grid=(1,),
        in_specs=[rows] * 5 + [whole((D, 3 * D))],
        out_specs=rows,
        out_shape=jax.ShapeDtypeStruct((ROWS, D), BF),
        compiler_params=params(),
        cost_estimate=cost(6 * ROWS * D * D, 14 * ROWS * D),
        name="inputs_back",
    )(ordered, dq, dk, dv, d_middle, w_qkv)


def qkv_back_kernel(ordered_ref, dq_ref, dk_ref, dv_ref, out_ref):
    normed, _ = norm_parts(ordered_ref[...].astype(F32))
    normed_t = normed.astype(BF).astype(F32).T.astype(BF)
    for at, ref in enumerate((dq_ref, dk_ref, dv_ref)):
        out_ref[:, at * D : (at + 1) * D] = dot(normed_t, ref[...]).astype(BF)


def qkv_back(ordered, dq, dk, dv):
    rows = whole((ROWS, D))
    return pl.pallas_call(
        qkv_back_kernel,
        grid=(1,),
        in_specs=[rows] * 4,
        out_specs=whole((D, 3 * D)),
        out_shape=jax.ShapeDtypeStruct((D, 3 * D), BF),
        compiler_params=params(),
        cost_estimate=cost(6 * ROWS * D * D, 14 * ROWS * D),
        name="qkv_back",
    )(ordered, dq, dk, dv)


def exchange(values):
    return lax.all_to_all(values, AXES, split_axis=0, concat_axis=0, tiled=True)


def total_of(values):
    return lax.psum(values, AXES)


def on_device(points, hilbert_pos, segment_ids, cotangent, w_qkv, w_proj, w_fc1, w_fc2):
    first_lane = ((lax.axis_index(AXES) % 4) * CAP).astype(jnp.int32).reshape(1)
    segment_row = segment_ids.reshape(1, ROWS)
    segment_column = segment_ids.reshape(ROWS, 1)
    wire, slot_row = pack_points(first_lane, hilbert_pos.reshape(1, ROWS), points)
    ordered, packed, landing = land_points(exchange(wire), w_qkv)
    up_received = exchange(pack_rows(slot_row, cotangent))
    mixed, exact, level = attend(segment_column, segment_row, packed)
    upstream = land_rows(landing, up_received)
    block, d_middle, d_mixed, d_proj, d_w1, d_w2 = mlp(
        ordered, mixed, upstream, w_proj, w_fc1, w_fc2
    )
    output_home = exchange(return_rows(landing, block))
    total_proj, total_w1, total_w2 = total_of((d_proj, d_w1, d_w2))
    dq, dk, dv = attend_back(segment_column, segment_row, packed, d_mixed, exact, level)
    grad_home = exchange(
        return_rows(landing, inputs_back(ordered, dq, dk, dv, d_middle, w_qkv))
    )
    d_qkv, total_w2 = lax.optimization_barrier((qkv_back(ordered, dq, dk, dv), total_w2))
    total_qkv = total_of(d_qkv)
    output = unpack_rows(slot_row, output_home)
    grad_points = unpack_rows(slot_row, grad_home)
    return (
        output,
        grad_points,
        total_qkv.astype(F32),
        total_proj.astype(F32),
        total_w1.astype(F32),
        total_w2.astype(F32),
    )


def solution(mesh):
    placed = (P(AXES, None), P(AXES), P(AXES), P(AXES, None), P(), P(), P(), P())
    return jax.shard_map(
        on_device,
        mesh=mesh,
        in_specs=placed,
        out_specs=(P(AXES, None), P(AXES, None), P(), P(), P(), P()),
        check_vma=False,
    )
```

```python
import math

import jax
import jax.numpy as jnp
from jax import lax
from jax.experimental import pallas as pl
from jax.experimental.pallas import tpu as pltpu
from jax.sharding import PartitionSpec as P

AXES = ("blk", "sub")
ROWS = 1024
D = 384
FF = 1536
LANES = 128
HEAD_DIM = 32
GROUPS = D // LANES
HEADS_PER_GROUP = LANES // HEAD_DIM
SHARDS = 128
CAP = 32
SLOTS = SHARDS * CAP
STEP_SHARDS = 32
STEP_SLOTS = STEP_SHARDS * CAP
STEPS = SHARDS // STEP_SHARDS
WIRE_ROWS = 3 * CAP + 2
EPSILON = 1e-05
SCALING = 1.0 / math.sqrt(HEAD_DIM)
LOG2E = 1.4426950408889634
MASKED = -1e30
TILE = 256
BF = jnp.bfloat16
F32 = jnp.float32
VMEM_LIMIT = 56 * 1024 * 1024

NO_COST = pl.CostEstimate(flops=1, bytes_accessed=1, transcendentals=0)

NT = (((1,), (1,)), ((), ()))


def dot(a, b):
    return jnp.dot(a, b, preferred_element_type=F32)


def dot_nt(a, b):
    return lax.dot_general(a, b, NT, preferred_element_type=F32)


def iota(shape, axis):
    return lax.broadcasted_iota(jnp.int32, shape, axis)


def params(grid_dims=1):
    return pltpu.CompilerParams(
        vmem_limit_bytes=VMEM_LIMIT,
        dimension_semantics=("arbitrary",) * grid_dims,
    )


def row_to_column(row):
    return jnp.broadcast_to(row, (8, row.shape[1])).T[:, 0:1]


def one_hot_slots(slot_row, first):
    ids = iota((STEP_SLOTS, ROWS), 0) + first
    return (ids == slot_row).astype(F32).astype(BF)


def pack_points_kernel(lane_ref, pos_ref, x_ref, out_ref, slot_ref, high_s, low_s):
    step = pl.program_id(0)

    @pl.when(step == 0)
    def _():
        pos = pos_ref[...]
        target = pos >> 10
        offset = pos & (ROWS - 1)
        member = iota((SHARDS, ROWS), 0) == target
        member_bf = member.astype(F32).astype(BF)
        before = (iota((ROWS, ROWS), 0) < iota((ROWS, ROWS), 1)).astype(F32).astype(BF)
        earlier = dot(member_bf, before)
        rank = jnp.sum(jnp.where(member, earlier, 0.0), axis=0, keepdims=True).astype(jnp.int32)
        slot_ref[...] = target * CAP + rank
        lane = (iota((LANES, ROWS), 0) == rank + lane_ref[0]).astype(F32).astype(BF)
        high = ((offset >> 5) + 1).astype(F32)
        low = (offset & 31).astype(F32)
        high_s[...] = dot_nt(jnp.where(member, high, 0.0).astype(BF), lane)
        low_s[...] = dot_nt(jnp.where(member, low, 0.0).astype(BF), lane)

    picked = dot(one_hot_slots(slot_ref[...], step * STEP_SLOTS), x_ref[...]).astype(BF)
    for piece in range(3):
        out_ref[:, piece * CAP : (piece + 1) * CAP, :] = picked[
            :, piece * LANES : (piece + 1) * LANES
        ].reshape(STEP_SHARDS, CAP, LANES)
    first = pl.multiple_of(step * STEP_SHARDS, STEP_SHARDS)
    high = high_s[pl.ds(first, STEP_SHARDS), :]
    low = low_s[pl.ds(first, STEP_SHARDS), :]
    for s in range(STEP_SHARDS):
        pair = jnp.concatenate([high[s : s + 1], low[s : s + 1]], axis=0)
        out_ref[s, 3 * CAP : WIRE_ROWS, :] = pair.astype(BF)


def pack_points(first_lane, pos_row, points):
    return pl.pallas_call(
        pack_points_kernel,
        grid=(STEPS,),
        in_specs=[
            pl.BlockSpec(memory_space=pltpu.SMEM),
            pl.BlockSpec((1, ROWS), lambda i: (0, 0)),
            pl.BlockSpec((ROWS, D), lambda i: (0, 0)),
        ],
        out_specs=[
            pl.BlockSpec((STEP_SHARDS, WIRE_ROWS, LANES), lambda i: (i, 0, 0)),
            pl.BlockSpec((1, ROWS), lambda i: (0, 0)),
        ],
        out_shape=[
            jax.ShapeDtypeStruct((SHARDS, WIRE_ROWS, LANES), BF),
            jax.ShapeDtypeStruct((1, ROWS), jnp.int32),
        ],
        scratch_shapes=[pltpu.VMEM((SHARDS, LANES), F32), pltpu.VMEM((SHARDS, LANES), F32)],
        compiler_params=params(),
        cost_estimate=NO_COST,
        name="pack_points",
    )(first_lane, pos_row, points)


def pack_rows_kernel(slot_ref, x_ref, out_ref):
    picked = dot(one_hot_slots(slot_ref[...], pl.program_id(0) * STEP_SLOTS), x_ref[...])
    out_ref[...] = picked.astype(BF).reshape(STEP_SHARDS, CAP, D)


def pack_rows(slot_row, values):
    return pl.pallas_call(
        pack_rows_kernel,
        grid=(STEPS,),
        in_specs=[
            pl.BlockSpec((1, ROWS), lambda i: (0, 0)),
            pl.BlockSpec((ROWS, D), lambda i: (0, 0)),
        ],
        out_specs=pl.BlockSpec((STEP_SHARDS, CAP, D), lambda i: (i, 0, 0)),
        out_shape=jax.ShapeDtypeStruct((SHARDS, CAP, D), BF),
        compiler_params=params(),
        cost_estimate=NO_COST,
        name="pack_rows",
    )(slot_row, values)


def unpack_rows_kernel(slot_ref, home_ref, out_ref, column_s, total_s):
    step = pl.program_id(0)

    @pl.when(step == 0)
    def _():
        column_s[...] = jnp.broadcast_to(
            row_to_column(slot_ref[...].astype(F32)).astype(jnp.int32), (ROWS, LANES)
        )
        total_s[...] = jnp.zeros_like(total_s)

    wide = jnp.concatenate([column_s[...]] * (STEP_SLOTS // LANES), axis=1)
    hot = (iota((ROWS, STEP_SLOTS), 1) + step * STEP_SLOTS == wide).astype(F32).astype(BF)
    total_s[...] += dot(hot, home_ref[...].reshape(STEP_SLOTS, D))

    @pl.when(step == STEPS - 1)
    def _():
        out_ref[...] = total_s[...].astype(BF)


def unpack_rows(slot_row, home):
    return pl.pallas_call(
        unpack_rows_kernel,
        grid=(STEPS,),
        in_specs=[
            pl.BlockSpec((1, ROWS), lambda i: (0, 0)),
            pl.BlockSpec((STEP_SHARDS, CAP, D), lambda i: (i, 0, 0)),
        ],
        out_specs=pl.BlockSpec((ROWS, D), lambda i: (0, 0)),
        out_shape=jax.ShapeDtypeStruct((ROWS, D), BF),
        scratch_shapes=[pltpu.VMEM((ROWS, LANES), jnp.int32), pltpu.VMEM((ROWS, D), F32)],
        compiler_params=params(),
        cost_estimate=NO_COST,
        name="unpack_rows",
    )(slot_row, home)


def norm_parts(values):
    centred = values - jnp.mean(values, axis=-1, keepdims=True)
    spread = jnp.mean(centred * centred, axis=-1, keepdims=True)
    scale = lax.rsqrt(spread + EPSILON)
    return centred * scale, scale


def norm_pull(normed, scale, upstream):
    across = jnp.mean(upstream, axis=-1, keepdims=True)
    along = jnp.mean(upstream * normed, axis=-1, keepdims=True)
    return scale * (upstream - across - normed * along)


def landing_one_hot(landing):
    return (iota((ROWS, STEP_SLOTS), 0) == landing).astype(F32).astype(BF)


def land_points_kernel(recv_ref, w_ref, ordered_ref, packed_ref, landing_ref, total_s):
    step = pl.program_id(0)

    @pl.when(step == 0)
    def _():
        total_s[...] = jnp.zeros_like(total_s)

    pieces = []
    for group in range(STEP_SHARDS // 4):
        pair = recv_ref[4 * group, 3 * CAP : WIRE_ROWS, :].astype(F32)
        for other in range(1, 4):
            pair = pair + recv_ref[4 * group + other, 3 * CAP : WIRE_ROWS, :].astype(F32)
        pieces.append((pair[0:1] - 1.0) * 32.0 + pair[1:2])
    landing = jnp.concatenate(pieces, axis=1).astype(jnp.int32)
    landing_ref[0] = landing
    rows = jnp.concatenate(
        [
            recv_ref[:, piece * CAP : (piece + 1) * CAP, :].reshape(STEP_SLOTS, LANES)
            for piece in range(3)
        ],
        axis=1,
    )
    total_s[...] += dot(landing_one_hot(landing), rows)

    @pl.when(step == STEPS - 1)
    def _():
        ordered = total_s[...]
        ordered_ref[...] = ordered.astype(BF)
        normed, _ = norm_parts(ordered)
        packed_ref[...] = dot(normed.astype(BF), w_ref[...]).astype(BF)


def land_points(received, w_qkv):
    return pl.pallas_call(
        land_points_kernel,
        grid=(STEPS,),
        in_specs=[
            pl.BlockSpec((STEP_SHARDS, WIRE_ROWS, LANES), lambda i: (i, 0, 0)),
            pl.BlockSpec((D, 3 * D), lambda i: (0, 0)),
        ],
        out_specs=[
            pl.BlockSpec((ROWS, D), lambda i: (0, 0)),
            pl.BlockSpec((ROWS, 3 * D), lambda i: (0, 0)),
            pl.BlockSpec((1, 1, STEP_SLOTS), lambda i: (i, 0, 0)),
        ],
        out_shape=[
            jax.ShapeDtypeStruct((ROWS, D), BF),
            jax.ShapeDtypeStruct((ROWS, 3 * D), BF),
            jax.ShapeDtypeStruct((STEPS, 1, STEP_SLOTS), jnp.int32),
        ],
        scratch_shapes=[pltpu.VMEM((ROWS, D), F32)],
        compiler_params=params(),
        cost_estimate=NO_COST,
        name="land_points",
    )(received, w_qkv)


def land_rows_kernel(landing_ref, recv_ref, out_ref, total_s):
    step = pl.program_id(0)

    @pl.when(step == 0)
    def _():
        total_s[...] = jnp.zeros_like(total_s)

    total_s[...] += dot(landing_one_hot(landing_ref[0]), recv_ref[...].reshape(STEP_SLOTS, D))

    @pl.when(step == STEPS - 1)
    def _():
        out_ref[...] = total_s[...].astype(BF)


def land_rows(landing, received):
    return pl.pallas_call(
        land_rows_kernel,
        grid=(STEPS,),
        in_specs=[
            pl.BlockSpec((1, 1, STEP_SLOTS), lambda i: (i, 0, 0)),
            pl.BlockSpec((STEP_SHARDS, CAP, D), lambda i: (i, 0, 0)),
        ],
        out_specs=pl.BlockSpec((ROWS, D), lambda i: (0, 0)),
        out_shape=jax.ShapeDtypeStruct((ROWS, D), BF),
        scratch_shapes=[pltpu.VMEM((ROWS, D), F32)],
        compiler_params=params(),
        cost_estimate=NO_COST,
        name="land_rows",
    )(landing, received)


def return_one_hot(landing):
    column = row_to_column(landing.astype(F32)).astype(jnp.int32)
    return (iota((STEP_SLOTS, ROWS), 1) == column).astype(F32).astype(BF)


def return_rows_kernel(landing_ref, x_ref, out_ref):
    picked = dot(return_one_hot(landing_ref[0]), x_ref[...])
    out_ref[...] = picked.astype(BF).reshape(STEP_SHARDS, CAP, D)


def return_rows(landing, values):
    return pl.pallas_call(
        return_rows_kernel,
        grid=(STEPS,),
        in_specs=[
            pl.BlockSpec((1, 1, STEP_SLOTS), lambda i: (i, 0, 0)),
            pl.BlockSpec((ROWS, D), lambda i: (0, 0)),
        ],
        out_specs=pl.BlockSpec((STEP_SHARDS, CAP, D), lambda i: (i, 0, 0)),
        out_shape=jax.ShapeDtypeStruct((SHARDS, CAP, D), BF),
        compiler_params=params(),
        cost_estimate=NO_COST,
        name="return_rows",
    )(landing, values)


def three_parts(values):
    high = values.astype(BF)
    rest = values - high.astype(F32)
    middle = rest.astype(BF)
    return high, middle, (rest - middle.astype(F32)).astype(BF)


def write_bias(bias_s, column_ref, row_ref):
    bias_s[...] = jnp.where(column_ref[...] == row_ref[...], 0.0, MASKED)


def head_of_lane():
    return iota((ROWS, LANES), 1) // HEAD_DIM


def roll_lanes(values, by):
    return pltpu.roll(values.astype(F32), by % LANES, 1)


def query_side(q, head, owner, shift=None):
    near, far = (head + 1) % HEADS_PER_GROUP, (head + 2) % HEADS_PER_GROUP
    high, middle, low = (part.astype(F32) for part in three_parts(q * (SCALING * LOG2E)))
    first = jnp.where(owner == head, high, 0.0)
    second = jnp.where(
        owner == near,
        roll_lanes(middle, HEAD_DIM),
        jnp.where(owner == far, roll_lanes(low, 2 * HEAD_DIM), 0.0),
    )
    if shift is not None:
        lane = iota((ROWS, LANES), 1) - head * HEAD_DIM
        parts = [part.astype(F32) for part in three_parts(-shift)]
        for at, part in enumerate(parts):
            second = jnp.where(lane == at, part, second)
    return jnp.concatenate([first.astype(BF), second.astype(BF)], axis=1)


def key_side(k, head, owner, shifted):
    near, far = (head + 1) % HEADS_PER_GROUP, (head + 2) % HEADS_PER_GROUP
    second = jnp.where(
        owner == near,
        roll_lanes(k, HEAD_DIM),
        jnp.where(owner == far, roll_lanes(k, 2 * HEAD_DIM), 0.0),
    )
    if shifted:
        lane = iota((ROWS, LANES), 1) - head * HEAD_DIM
        second = jnp.where((lane >= 0) & (lane < 3), 1.0, second)
    return jnp.concatenate([k.astype(BF), second.astype(BF)], axis=1)


def attend_kernel(column_ref, row_ref, q_ref, k_ref, v_ref, mixed_ref, exact_ref, level_ref, bias_s):
    @pl.when(pl.program_id(0) == 0)
    def _():
        write_bias(bias_s, column_ref, row_ref)

    owner = head_of_lane()
    q, k, v = (ref[...].astype(F32) for ref in (q_ref, k_ref, v_ref))
    owner_tile = owner[:TILE]
    for head in range(HEADS_PER_GROUP):
        queries = query_side(q, head, owner)
        keys = key_side(k, head, owner, False)
        values = jnp.concatenate(
            [jnp.where(owner == head, v, 0.0).astype(BF), jnp.ones((ROWS, LANES), BF)], axis=1
        )
        for tile in range(ROWS // TILE):
            rows = slice(tile * TILE, (tile + 1) * TILE)
            scores = dot_nt(queries[rows], keys) + bias_s[rows, :]
            most = jnp.max(scores, axis=-1, keepdims=True)
            raised = jnp.exp2(scores - most).astype(BF)
            both = dot(raised, values)
            total = both[:, LANES:]
            result = both[:, :LANES] / total
            level = most + jnp.log2(total)
            if head == 0:
                exact_ref[rows, :] = result
                level_ref[rows, :] = level
            else:
                mine = owner_tile == head
                exact_ref[rows, :] = jnp.where(mine, result, exact_ref[rows, :])
                level_ref[rows, :] = jnp.where(mine, level, level_ref[rows, :])
    mixed_ref[...] = exact_ref[...].astype(BF)


def group_spec(first=0):
    return pl.BlockSpec((ROWS, LANES), lambda g: (0, first + g))


def whole(shape):
    return pl.BlockSpec(shape, lambda g: (0,) * len(shape))


def attend(segment_column, segment_row, packed):
    return pl.pallas_call(
        attend_kernel,
        grid=(GROUPS,),
        in_specs=[
            whole((ROWS, 1)),
            whole((1, ROWS)),
            group_spec(0),
            group_spec(GROUPS),
            group_spec(2 * GROUPS),
        ],
        out_specs=[group_spec()] * 3,
        out_shape=[
            jax.ShapeDtypeStruct((ROWS, D), BF),
            jax.ShapeDtypeStruct((ROWS, D), F32),
            jax.ShapeDtypeStruct((ROWS, D), F32),
        ],
        scratch_shapes=[pltpu.VMEM((ROWS, ROWS), F32)],
        compiler_params=params(),
        cost_estimate=NO_COST,
        name="attend",
    )(segment_column, segment_row, packed, packed, packed)


def attend_back_kernel(
    column_ref,
    row_ref,
    q_ref,
    k_ref,
    v_ref,
    up_ref,
    exact_ref,
    level_ref,
    out_ref,
    bias_s,
    dqt_s,
    dk_s,
    dv_s,
):
    @pl.when(pl.program_id(0) == 0)
    def _():
        write_bias(bias_s, column_ref, row_ref)

    owner = head_of_lane()
    q, k, v, up = (ref[...].astype(F32) for ref in (q_ref, k_ref, v_ref, up_ref))
    level = level_ref[...]
    keys_t = k.T.astype(BF)
    from_head = iota((LANES, LANES), 0) // HEAD_DIM
    to_head = iota((LANES, LANES), 1) // HEAD_DIM
    spread = ((from_head + 1) % HEADS_PER_GROUP == to_head).astype(F32).astype(BF)
    delta = sum(dot(part, spread) for part in three_parts(up * exact_ref[...]))
    delta_parts = [part.astype(F32) for part in three_parts(-delta)]
    for head in range(HEADS_PER_GROUP):
        mine = owner == head
        near = (head + 1) % HEADS_PER_GROUP
        lane = iota((ROWS, LANES), 1) - near * HEAD_DIM
        queries = query_side(q, head, owner, level)
        keys = key_side(k, head, owner, True)
        up_mine = jnp.where(mine, up, 0.0)
        up_side = up_mine
        for at, part in enumerate(delta_parts):
            up_side = jnp.where(lane == at, part, up_side)
        up_side = up_side.astype(BF)
        up_mine = up_mine.astype(BF)
        value_side = jnp.where((lane >= 0) & (lane < 3), 1.0, v).astype(BF)
        query_mine = jnp.where(mine, q, 0.0).astype(BF)
        head_rows = slice(head * HEAD_DIM, (head + 1) * HEAD_DIM)
        for tile in range(ROWS // TILE):
            rows = slice(tile * TILE, (tile + 1) * TILE)
            weights = jnp.exp2(dot_nt(keys[rows], queries) + bias_s[rows, :])
            pulled = weights * dot_nt(value_side[rows], up_side)
            pulled = pulled.astype(BF)
            dv_part = dot(weights.astype(BF), up_mine)
            dk_part = dot(pulled, query_mine)
            dq_part = dot(keys_t[head_rows, rows], pulled)
            if head == 0:
                dv_s[rows, :] = dv_part
                dk_s[rows, :] = dk_part
            else:
                dv_s[rows, :] += dv_part
                dk_s[rows, :] += dk_part
            if tile == 0:
                dqt_s[head_rows, :] = dq_part
            else:
                dqt_s[head_rows, :] += dq_part
    out_ref[:, :LANES] = (dqt_s[...] * SCALING).T.astype(BF)
    out_ref[:, LANES : 2 * LANES] = (dk_s[...] * SCALING).astype(BF)
    out_ref[:, 2 * LANES :] = dv_s[...].astype(BF)


def attend_back(segment_column, segment_row, packed, upstream, exact, level):
    return pl.pallas_call(
        attend_back_kernel,
        grid=(GROUPS,),
        in_specs=[
            whole((ROWS, 1)),
            whole((1, ROWS)),
            group_spec(0),
            group_spec(GROUPS),
            group_spec(2 * GROUPS),
            group_spec(),
            group_spec(),
            group_spec(),
        ],
        out_specs=pl.BlockSpec((ROWS, 3 * LANES), lambda g: (0, g)),
        out_shape=jax.ShapeDtypeStruct((ROWS, 3 * D), BF),
        scratch_shapes=[
            pltpu.VMEM((ROWS, ROWS), F32),
            pltpu.VMEM((LANES, ROWS), F32),
            pltpu.VMEM((ROWS, LANES), F32),
            pltpu.VMEM((ROWS, LANES), F32),
        ],
        compiler_params=params(),
        cost_estimate=NO_COST,
        name="attend_back",
    )(segment_column, segment_row, packed, packed, packed, upstream, exact, level)


FORWARD_STEP = 512
BACK_STEP = 384


def mlp_kernel(
    ordered_ref,
    mixed_ref,
    w_proj_ref,
    w1_ref,
    w2_ref,
    block_ref,
    middle_ref,
    hidden_ref,
    slope_ref,
    normed_s,
    out_s,
):
    step = pl.program_id(0)

    @pl.when(step == 0)
    def _():
        middle = (
            ordered_ref[...].astype(F32) + dot(mixed_ref[...], w_proj_ref[...])
        ).astype(BF)
        middle_ref[...] = middle
        normed, _ = norm_parts(middle.astype(F32))
        normed_s[...] = normed.astype(BF)
        out_s[...] = middle.astype(F32)

    before = dot(normed_s[...], w1_ref[...])
    half = 0.5 * (1.0 + lax.erf(before * math.sqrt(0.5)))
    density = jnp.exp(before * before * -0.5) * (1.0 / math.sqrt(2.0 * math.pi))
    hidden = (before * half).astype(BF)
    hidden_ref[...] = hidden
    slope_ref[...] = half + before * density
    out_s[...] += dot(hidden, w2_ref[...])

    @pl.when(step == FF // FORWARD_STEP - 1)
    def _():
        block_ref[...] = out_s[...].astype(BF)


def mlp(ordered, mixed, w_proj, w_fc1, w_fc2):
    rows = whole((ROWS, D))
    wide = pl.BlockSpec((ROWS, FORWARD_STEP), lambda i: (0, i))
    return pl.pallas_call(
        mlp_kernel,
        grid=(FF // FORWARD_STEP,),
        in_specs=[
            rows,
            rows,
            whole((D, D)),
            pl.BlockSpec((D, FORWARD_STEP), lambda i: (0, i)),
            pl.BlockSpec((FORWARD_STEP, D), lambda i: (i, 0)),
        ],
        out_specs=[rows, rows, wide, wide],
        out_shape=[
            jax.ShapeDtypeStruct((ROWS, D), BF),
            jax.ShapeDtypeStruct((ROWS, D), BF),
            jax.ShapeDtypeStruct((ROWS, FF), BF),
            jax.ShapeDtypeStruct((ROWS, FF), F32),
        ],
        scratch_shapes=[pltpu.VMEM((ROWS, D), BF), pltpu.VMEM((ROWS, D), F32)],
        compiler_params=params(),
        cost_estimate=NO_COST,
        name="mlp",
    )(ordered, mixed, w_proj, w_fc1, w_fc2)


def mlp_back_kernel(
    up_ref,
    middle_ref,
    mixed_ref,
    hidden_ref,
    slope_ref,
    w_proj_ref,
    w1_ref,
    w2_ref,
    d_middle_ref,
    d_mixed_ref,
    d_proj_ref,
    d_w1_ref,
    d_w2_ref,
    normed_t_s,
    up_t_s,
    d_normed_s,
):
    step = pl.program_id(0)
    up = up_ref[...]

    @pl.when(step == 0)
    def _():
        normed, _ = norm_parts(middle_ref[...].astype(F32))
        normed_t_s[...] = normed.astype(BF).astype(F32).T.astype(BF)
        up_t_s[...] = up.astype(F32).T.astype(BF)
        d_normed_s[...] = jnp.zeros_like(d_normed_s)

    d_hidden = dot_nt(up, w2_ref[...]).astype(BF).astype(F32)
    d_before = (d_hidden * slope_ref[...]).astype(BF)
    d_w2_ref[...] = dot(up_t_s[...], hidden_ref[...]).T.astype(BF)
    d_w1_ref[...] = dot(normed_t_s[...], d_before).astype(BF)
    d_normed_s[...] += dot_nt(d_before, w1_ref[...])

    @pl.when(step == FF // BACK_STEP - 1)
    def _():
        normed, scale = norm_parts(middle_ref[...].astype(F32))
        pulled = norm_pull(normed, scale, d_normed_s[...].astype(BF).astype(F32)).astype(BF)
        d_middle = (up.astype(F32) + pulled.astype(F32)).astype(BF)
        d_middle_ref[...] = d_middle
        d_mixed_ref[...] = dot_nt(d_middle, w_proj_ref[...]).astype(BF)
        d_proj_ref[...] = dot(mixed_ref[...].astype(F32).T.astype(BF), d_middle).astype(BF)


def mlp_back(upstream, middle, mixed, hidden, slope, w_proj, w_fc1, w_fc2):
    rows = whole((ROWS, D))
    wide = pl.BlockSpec((ROWS, BACK_STEP), lambda i: (0, i))
    down = pl.BlockSpec((BACK_STEP, D), lambda i: (i, 0))
    return pl.pallas_call(
        mlp_back_kernel,
        grid=(FF // BACK_STEP,),
        in_specs=[
            rows,
            rows,
            rows,
            wide,
            wide,
            whole((D, D)),
            pl.BlockSpec((D, BACK_STEP), lambda i: (0, i)),
            down,
        ],
        out_specs=[rows, rows, whole((D, D)), down, down],
        out_shape=[
            jax.ShapeDtypeStruct((ROWS, D), BF),
            jax.ShapeDtypeStruct((ROWS, D), BF),
            jax.ShapeDtypeStruct((D, D), BF),
            jax.ShapeDtypeStruct((FF, D), BF),
            jax.ShapeDtypeStruct((FF, D), BF),
        ],
        scratch_shapes=[
            pltpu.VMEM((D, ROWS), BF),
            pltpu.VMEM((D, ROWS), BF),
            pltpu.VMEM((ROWS, D), F32),
        ],
        compiler_params=params(),
        cost_estimate=NO_COST,
        name="mlp_back",
    )(upstream, middle, mixed, hidden, slope, w_proj, w_fc1, w_fc2)


def group_columns(part, group):
    first = part * D + group * LANES
    return slice(first, first + LANES)


def inputs_back_kernel(ordered_ref, d_packed_ref, d_middle_ref, w_ref, out_ref):
    normed, scale = norm_parts(ordered_ref[...].astype(F32))
    weights = jnp.concatenate(
        [
            w_ref[:, group_columns(part, group)]
            for group in range(GROUPS)
            for part in range(3)
        ],
        axis=1,
    )
    d_normed = dot_nt(d_packed_ref[...], weights)
    pulled = norm_pull(normed, scale, d_normed.astype(BF).astype(F32)).astype(BF)
    out_ref[...] = (d_middle_ref[...].astype(F32) + pulled.astype(F32)).astype(BF)


def inputs_back(ordered, d_packed, d_middle, w_qkv):
    rows = whole((ROWS, D))
    return pl.pallas_call(
        inputs_back_kernel,
        grid=(1,),
        in_specs=[rows, whole((ROWS, 3 * D)), rows, whole((D, 3 * D))],
        out_specs=rows,
        out_shape=jax.ShapeDtypeStruct((ROWS, D), BF),
        compiler_params=params(),
        cost_estimate=NO_COST,
        name="inputs_back",
    )(ordered, d_packed, d_middle, w_qkv)


def qkv_back_kernel(ordered_ref, d_packed_ref, proj_ref, out_ref):
    normed, _ = norm_parts(ordered_ref[...].astype(F32))
    normed_t = normed.astype(BF).astype(F32).T.astype(BF)
    for group in range(GROUPS):
        columns = slice(group * D, (group + 1) * D)
        out_ref[columns, :] = dot(normed_t, d_packed_ref[:, columns]).astype(BF)
    out_ref[GROUPS * D :, :] = proj_ref[...]


def qkv_back(ordered, d_packed, d_proj):
    return pl.pallas_call(
        qkv_back_kernel,
        grid=(1,),
        in_specs=[whole((ROWS, D)), whole((ROWS, 3 * D)), whole((D, D))],
        out_specs=whole(((GROUPS + 1) * D, D)),
        out_shape=jax.ShapeDtypeStruct(((GROUPS + 1) * D, D), BF),
        compiler_params=params(),
        cost_estimate=NO_COST,
        name="qkv_back",
    )(ordered, d_packed, d_proj)


def place(axis):
    name, stride, size = {
        "y": ("blk", 2, 4),
        "core": ("blk", 1, 2),
        "x": ("sub", 4, 4),
        "z": ("sub", 1, 4),
    }[axis]
    return name, stride, size


def swap(values, axis, kind):
    name, stride, size = place(axis)
    pairs = []
    for index in range(lax.axis_size(name)):
        c = index // stride % size
        partner = 3 - c if kind else c ^ 1
        pairs.append((index, index + (partner - c) * stride))
    return lax.ppermute(values, name, pairs)


def side(axis, kind):
    name, stride, size = place(axis)
    c = lax.axis_index(name) // stride % size
    return c >> 1 if kind else (c ^ (c >> 1)) & 1


def add(a, b):
    return (a.astype(F32) + b.astype(F32)).astype(BF)


def halve_begin(values, axis, kind):
    keep = side(axis, kind)
    half = values.shape[0] // 2
    own = lax.dynamic_slice_in_dim(values, keep * half, half, 0)
    away = lax.dynamic_slice_in_dim(values, (1 - keep) * half, half, 0)
    return own, swap(away, axis, kind)


def halve(values, axis, kind):
    return add(*halve_begin(values, axis, kind))


def meet_begin(values, axis, kind):
    return values, swap(values, axis, kind)


def meet(values, axis, kind):
    return add(*meet_begin(values, axis, kind))


def double(values, axis, kind):
    keep = side(axis, kind)
    half = values.shape[0]
    other = swap(values, axis, kind)
    both = jnp.zeros((2 * half,) + values.shape[1:], values.dtype)
    both = lax.dynamic_update_slice_in_dim(both, values, keep * half, 0)
    return lax.dynamic_update_slice_in_dim(both, other, (1 - keep) * half, 0)


def spread_again(values, axis):
    for kind in (1, 0):
        values = double(values, axis, kind)
    return values


def finish_kernel(
    keep_ref, w1_ref, w1_other_ref, w2_ref, w2_other_ref, rest_ref, rest_other_ref, qkv_ref, proj_ref, out1_ref, out2_ref
):
    step = pl.program_id(0)
    rows = pl.ds(pl.multiple_of(lax.rem(step, 2) * D, D), D)
    own = step // 2 == keep_ref[0]

    def block(mine_ref, other_ref):
        return jnp.where(own, mine_ref[rows, :].astype(F32), other_ref[rows, :].astype(F32))

    out1_ref[...] = block(w1_ref, w1_other_ref)
    out2_ref[...] = block(w2_ref, w2_other_ref)
    rest = block(rest_ref, rest_other_ref)
    for group in range(GROUPS):

        @pl.when(step == group)
        def _(group=group):
            for part in range(3):
                qkv_ref[:, group_columns(part, group)] = rest[:, part * LANES : (part + 1) * LANES]

    @pl.when(step == GROUPS)
    def _():
        proj_ref[...] = rest


def finish(sums):
    keep = side("core", 0).astype(jnp.int32).reshape(1)
    halves = [part for mine in sums for part in (mine, swap(mine, "core", 0))]
    half = whole((FF // 2, D))
    return pl.pallas_call(
        finish_kernel,
        grid=(FF // D,),
        in_specs=[pl.BlockSpec(memory_space=pltpu.SMEM)] + [half] * 6,
        out_specs=[
            whole((D, 3 * D)),
            whole((D, D)),
            pl.BlockSpec((D, D), lambda i: (0, i)),
            pl.BlockSpec((D, D), lambda i: (i, 0)),
        ],
        out_shape=[
            jax.ShapeDtypeStruct((D, 3 * D), F32),
            jax.ShapeDtypeStruct((D, D), F32),
            jax.ShapeDtypeStruct((D, FF), F32),
            jax.ShapeDtypeStruct((FF, D), F32),
        ],
        compiler_params=params(),
        cost_estimate=NO_COST,
        name="finish",
    )(keep, *halves)


together = lax.optimization_barrier


def exchange(values):
    return lax.all_to_all(values, AXES, split_axis=0, concat_axis=0, tiled=True)


def on_device(points, hilbert_pos, segment_ids, cotangent, w_qkv, w_proj, w_fc1, w_fc2):
    first_lane = ((lax.axis_index(AXES) % 4) * CAP).astype(jnp.int32).reshape(1)
    segment_row = segment_ids.reshape(1, ROWS)
    segment_column = segment_ids.reshape(ROWS, 1)
    wire, slot_row = pack_points(first_lane, hilbert_pos.reshape(1, ROWS), points)
    ordered, packed, landing = land_points(exchange(wire), w_qkv)
    up_received = exchange(pack_rows(slot_row, cotangent))
    mixed, exact, level = attend(segment_column, segment_row, packed)
    block, middle, hidden, slope = mlp(ordered, mixed, w_proj, w_fc1, w_fc2)
    returned, up_received = together((return_rows(landing, block), up_received))
    output_home = exchange(returned)
    upstream = land_rows(landing, up_received)
    d_middle, d_mixed, d_proj, d_w1, d_w2 = mlp_back(
        upstream, middle, mixed, hidden, slope, w_proj, w_fc1, w_fc2
    )
    sum1, sum2 = halve(d_w1, "core", 0), halve(d_w2, "core", 0)
    sum1, sum2, d_mixed = together((sum1, sum2, d_mixed))
    sum1, sum2 = halve_begin(sum1, "y", 0), halve_begin(sum2, "x", 0)
    d_packed = attend_back(segment_column, segment_row, packed, d_mixed, exact, level)
    sum1, sum2, d_packed, output_home = together((sum1, sum2, d_packed, output_home))
    sum1, sum2 = halve_begin(add(*sum1), "y", 1), halve_begin(add(*sum2), "x", 1)
    d_inputs = inputs_back(ordered, d_packed, d_middle, w_qkv)
    sum1, sum2, d_inputs = together((sum1, sum2, d_inputs))
    sum1, sum2 = meet_begin(add(*sum1), "x", 0), meet_begin(add(*sum2), "z", 0)
    back = return_rows(landing, d_inputs)
    grad_home = exchange(back)
    sum1, sum2, d_packed, _ = together((sum1, sum2, d_packed, back))
    output_home, _ = together((output_home, back))
    sum3 = halve_begin(qkv_back(ordered, d_packed, d_proj), "core", 0)
    sum1, sum2 = meet(add(*sum1), "x", 1), meet(add(*sum2), "z", 1)
    output = unpack_rows(slot_row, output_home)
    sum1, sum2, sum3, output = together((sum1, sum2, sum3, output))
    sum1, sum2 = meet(sum1, "z", 0), meet(sum2, "y", 0)
    sum1, sum2 = meet(sum1, "z", 1), meet(sum2, "y", 1)
    sum3 = halve(halve(add(*sum3), "z", 0), "z", 1)
    for axis in ("y", "x"):
        for kind in (0, 1):
            sum3 = meet(sum3, axis, kind)
    sum1, sum2 = spread_again(sum1, "y"), spread_again(sum2, "x")
    sum1, sum2, sum3, grad_home = together((sum1, sum2, sum3, grad_home))
    total_qkv, total_proj, total_w1, total_w2 = finish((sum1, sum2, spread_again(sum3, "z")))
    grad_points = unpack_rows(slot_row, grad_home)
    return output, grad_points, total_qkv, total_proj, total_w1, total_w2


def solution(mesh):
    placed = (P(AXES, None), P(AXES), P(AXES), P(AXES, None), P(), P(), P(), P())
    return jax.shard_map(
        on_device,
        mesh=mesh,
        in_specs=placed,
        out_specs=(P(AXES, None), P(AXES, None), P(), P(), P(), P()),
        check_vma=False,
    )
```

```python
import math

import jax
import jax.numpy as jnp
from jax import lax
from jax.experimental import pallas as pl
from jax.experimental.pallas import tpu as pltpu
from jax.sharding import PartitionSpec as P

AXES = ("blk", "sub")
ROWS = 1024
D = 384
FF = 1536
LANES = 128
HEAD_DIM = 32
GROUPS = D // LANES
HEADS_PER_GROUP = LANES // HEAD_DIM
SHARDS = 128
CAP = 32
SLOTS = SHARDS * CAP
STEP_SHARDS = 32
STEP_SLOTS = STEP_SHARDS * CAP
STEPS = SHARDS // STEP_SHARDS
WIRE_ROWS = 3 * CAP + 2
EPSILON = 1e-05
SCALING = 1.0 / math.sqrt(HEAD_DIM)
LOG2E = 1.4426950408889634
MASKED = -1e30
TILE = 256
BF = jnp.bfloat16
F32 = jnp.float32
VMEM_LIMIT = 56 * 1024 * 1024

NO_COST = pl.CostEstimate(flops=1, bytes_accessed=1, transcendentals=0)

NT = (((1,), (1,)), ((), ()))


def dot(a, b):
    return jnp.dot(a, b, preferred_element_type=F32)


def dot_nt(a, b):
    return lax.dot_general(a, b, NT, preferred_element_type=F32)


def iota(shape, axis):
    return lax.broadcasted_iota(jnp.int32, shape, axis)


def params(grid_dims=1):
    return pltpu.CompilerParams(
        vmem_limit_bytes=VMEM_LIMIT,
        dimension_semantics=("arbitrary",) * grid_dims,
    )


def row_to_column(row):
    return jnp.broadcast_to(row, (8, row.shape[1])).T[:, 0:1]


def one_hot_slots(slot_row, first):
    ids = iota((STEP_SLOTS, ROWS), 0) + first
    return (ids == slot_row).astype(F32).astype(BF)


def pack_points_kernel(lane_ref, pos_ref, x_ref, out_ref, slot_ref, high_s, low_s):
    step = pl.program_id(0)

    @pl.when(step == 0)
    def _():
        pos = pos_ref[...]
        target = pos >> 10
        offset = pos & (ROWS - 1)
        member = iota((SHARDS, ROWS), 0) == target
        member_bf = member.astype(F32).astype(BF)
        before = (iota((ROWS, ROWS), 0) < iota((ROWS, ROWS), 1)).astype(F32).astype(BF)
        earlier = dot(member_bf, before)
        rank = jnp.sum(jnp.where(member, earlier, 0.0), axis=0, keepdims=True).astype(jnp.int32)
        slot_ref[...] = target * CAP + rank
        lane = (iota((LANES, ROWS), 0) == rank + lane_ref[0]).astype(F32).astype(BF)
        high = ((offset >> 5) + 1).astype(F32)
        low = (offset & 31).astype(F32)
        high_s[...] = dot_nt(jnp.where(member, high, 0.0).astype(BF), lane)
        low_s[...] = dot_nt(jnp.where(member, low, 0.0).astype(BF), lane)

    picked = dot(one_hot_slots(slot_ref[...], step * STEP_SLOTS), x_ref[...]).astype(BF)
    for piece in range(3):
        out_ref[:, piece * CAP : (piece + 1) * CAP, :] = picked[
            :, piece * LANES : (piece + 1) * LANES
        ].reshape(STEP_SHARDS, CAP, LANES)
    first = pl.multiple_of(step * STEP_SHARDS, STEP_SHARDS)
    high = high_s[pl.ds(first, STEP_SHARDS), :]
    low = low_s[pl.ds(first, STEP_SHARDS), :]
    for s in range(STEP_SHARDS):
        pair = jnp.concatenate([high[s : s + 1], low[s : s + 1]], axis=0)
        out_ref[s, 3 * CAP : WIRE_ROWS, :] = pair.astype(BF)


def pack_points(first_lane, pos_row, points):
    return pl.pallas_call(
        pack_points_kernel,
        grid=(STEPS,),
        in_specs=[
            pl.BlockSpec(memory_space=pltpu.SMEM),
            pl.BlockSpec((1, ROWS), lambda i: (0, 0)),
            pl.BlockSpec((ROWS, D), lambda i: (0, 0)),
        ],
        out_specs=[
            pl.BlockSpec((STEP_SHARDS, WIRE_ROWS, LANES), lambda i: (i, 0, 0)),
            pl.BlockSpec((1, ROWS), lambda i: (0, 0)),
        ],
        out_shape=[
            jax.ShapeDtypeStruct((SHARDS, WIRE_ROWS, LANES), BF),
            jax.ShapeDtypeStruct((1, ROWS), jnp.int32),
        ],
        scratch_shapes=[pltpu.VMEM((SHARDS, LANES), F32), pltpu.VMEM((SHARDS, LANES), F32)],
        compiler_params=params(),
        cost_estimate=NO_COST,
        name="pack_points",
    )(first_lane, pos_row, points)


def pack_rows_kernel(slot_ref, x_ref, out_ref):
    picked = dot(one_hot_slots(slot_ref[...], pl.program_id(0) * STEP_SLOTS), x_ref[...])
    out_ref[...] = picked.astype(BF).reshape(STEP_SHARDS, CAP, D)


def pack_rows(slot_row, values):
    return pl.pallas_call(
        pack_rows_kernel,
        grid=(STEPS,),
        in_specs=[
            pl.BlockSpec((1, ROWS), lambda i: (0, 0)),
            pl.BlockSpec((ROWS, D), lambda i: (0, 0)),
        ],
        out_specs=pl.BlockSpec((STEP_SHARDS, CAP, D), lambda i: (i, 0, 0)),
        out_shape=jax.ShapeDtypeStruct((SHARDS, CAP, D), BF),
        compiler_params=params(),
        cost_estimate=NO_COST,
        name="pack_rows",
    )(slot_row, values)


def unpack_rows_kernel(slot_ref, home_ref, out_ref, column_s, total_s):
    step = pl.program_id(0)

    @pl.when(step == 0)
    def _():
        column_s[...] = jnp.broadcast_to(
            row_to_column(slot_ref[...].astype(F32)).astype(jnp.int32), (ROWS, LANES)
        )
        total_s[...] = jnp.zeros_like(total_s)

    wide = jnp.concatenate([column_s[...]] * (STEP_SLOTS // LANES), axis=1)
    hot = (iota((ROWS, STEP_SLOTS), 1) + step * STEP_SLOTS == wide).astype(F32).astype(BF)
    total_s[...] += dot(hot, home_ref[...].reshape(STEP_SLOTS, D))

    @pl.when(step == STEPS - 1)
    def _():
        out_ref[...] = total_s[...].astype(BF)


def unpack_rows(slot_row, home):
    return pl.pallas_call(
        unpack_rows_kernel,
        grid=(STEPS,),
        in_specs=[
            pl.BlockSpec((1, ROWS), lambda i: (0, 0)),
            pl.BlockSpec((STEP_SHARDS, CAP, D), lambda i: (i, 0, 0)),
        ],
        out_specs=pl.BlockSpec((ROWS, D), lambda i: (0, 0)),
        out_shape=jax.ShapeDtypeStruct((ROWS, D), BF),
        scratch_shapes=[pltpu.VMEM((ROWS, LANES), jnp.int32), pltpu.VMEM((ROWS, D), F32)],
        compiler_params=params(),
        cost_estimate=NO_COST,
        name="unpack_rows",
    )(slot_row, home)


def norm_parts(values):
    centred = values - jnp.mean(values, axis=-1, keepdims=True)
    spread = jnp.mean(centred * centred, axis=-1, keepdims=True)
    scale = lax.rsqrt(spread + EPSILON)
    return centred * scale, scale


def norm_pull(normed, scale, upstream):
    across = jnp.mean(upstream, axis=-1, keepdims=True)
    along = jnp.mean(upstream * normed, axis=-1, keepdims=True)
    return scale * (upstream - across - normed * along)


def landing_one_hot(landing):
    return (iota((ROWS, STEP_SLOTS), 0) == landing).astype(F32).astype(BF)


def land_points_kernel(recv_ref, w_ref, ordered_ref, packed_ref, landing_ref, total_s):
    step = pl.program_id(0)

    @pl.when(step == 0)
    def _():
        total_s[...] = jnp.zeros_like(total_s)

    pieces = []
    for group in range(STEP_SHARDS // 4):
        pair = recv_ref[4 * group, 3 * CAP : WIRE_ROWS, :].astype(F32)
        for other in range(1, 4):
            pair = pair + recv_ref[4 * group + other, 3 * CAP : WIRE_ROWS, :].astype(F32)
        pieces.append((pair[0:1] - 1.0) * 32.0 + pair[1:2])
    landing = jnp.concatenate(pieces, axis=1).astype(jnp.int32)
    landing_ref[0] = landing
    rows = jnp.concatenate(
        [
            recv_ref[:, piece * CAP : (piece + 1) * CAP, :].reshape(STEP_SLOTS, LANES)
            for piece in range(3)
        ],
        axis=1,
    )
    total_s[...] += dot(landing_one_hot(landing), rows)

    @pl.when(step == STEPS - 1)
    def _():
        ordered = total_s[...]
        ordered_ref[...] = ordered.astype(BF)
        normed, _ = norm_parts(ordered)
        packed_ref[...] = dot(normed.astype(BF), w_ref[...]).astype(BF)


def land_points(received, w_qkv):
    return pl.pallas_call(
        land_points_kernel,
        grid=(STEPS,),
        in_specs=[
            pl.BlockSpec((STEP_SHARDS, WIRE_ROWS, LANES), lambda i: (i, 0, 0)),
            pl.BlockSpec((D, 3 * D), lambda i: (0, 0)),
        ],
        out_specs=[
            pl.BlockSpec((ROWS, D), lambda i: (0, 0)),
            pl.BlockSpec((ROWS, 3 * D), lambda i: (0, 0)),
            pl.BlockSpec((1, 1, STEP_SLOTS), lambda i: (i, 0, 0)),
        ],
        out_shape=[
            jax.ShapeDtypeStruct((ROWS, D), BF),
            jax.ShapeDtypeStruct((ROWS, 3 * D), BF),
            jax.ShapeDtypeStruct((STEPS, 1, STEP_SLOTS), jnp.int32),
        ],
        scratch_shapes=[pltpu.VMEM((ROWS, D), F32)],
        compiler_params=params(),
        cost_estimate=NO_COST,
        name="land_points",
    )(received, w_qkv)


def land_rows_kernel(landing_ref, recv_ref, out_ref, total_s):
    step = pl.program_id(0)

    @pl.when(step == 0)
    def _():
        total_s[...] = jnp.zeros_like(total_s)

    total_s[...] += dot(landing_one_hot(landing_ref[0]), recv_ref[...].reshape(STEP_SLOTS, D))

    @pl.when(step == STEPS - 1)
    def _():
        out_ref[...] = total_s[...].astype(BF)


def land_rows(landing, received):
    return pl.pallas_call(
        land_rows_kernel,
        grid=(STEPS,),
        in_specs=[
            pl.BlockSpec((1, 1, STEP_SLOTS), lambda i: (i, 0, 0)),
            pl.BlockSpec((STEP_SHARDS, CAP, D), lambda i: (i, 0, 0)),
        ],
        out_specs=pl.BlockSpec((ROWS, D), lambda i: (0, 0)),
        out_shape=jax.ShapeDtypeStruct((ROWS, D), BF),
        scratch_shapes=[pltpu.VMEM((ROWS, D), F32)],
        compiler_params=params(),
        cost_estimate=NO_COST,
        name="land_rows",
    )(landing, received)


def return_one_hot(landing):
    column = row_to_column(landing.astype(F32)).astype(jnp.int32)
    return (iota((STEP_SLOTS, ROWS), 1) == column).astype(F32).astype(BF)


def return_rows_kernel(landing_ref, x_ref, out_ref):
    picked = dot(return_one_hot(landing_ref[0]), x_ref[...])
    out_ref[...] = picked.astype(BF).reshape(STEP_SHARDS, CAP, D)


def return_rows(landing, values):
    return pl.pallas_call(
        return_rows_kernel,
        grid=(STEPS,),
        in_specs=[
            pl.BlockSpec((1, 1, STEP_SLOTS), lambda i: (i, 0, 0)),
            pl.BlockSpec((ROWS, D), lambda i: (0, 0)),
        ],
        out_specs=pl.BlockSpec((STEP_SHARDS, CAP, D), lambda i: (i, 0, 0)),
        out_shape=jax.ShapeDtypeStruct((SHARDS, CAP, D), BF),
        compiler_params=params(),
        cost_estimate=NO_COST,
        name="return_rows",
    )(landing, values)


def three_parts(values):
    high = values.astype(BF)
    rest = values - high.astype(F32)
    middle = rest.astype(BF)
    return high, middle, (rest - middle.astype(F32)).astype(BF)


def write_bias(bias_s, column_ref, row_ref):
    bias_s[...] = jnp.where(column_ref[...] == row_ref[...], 0.0, MASKED)


def head_of_lane():
    return iota((ROWS, LANES), 1) // HEAD_DIM


def roll_lanes(values, by):
    return pltpu.roll(values.astype(F32), by % LANES, 1)


def query_side(q, head, owner, shift=None):
    near, far = (head + 1) % HEADS_PER_GROUP, (head + 2) % HEADS_PER_GROUP
    high, middle, low = (part.astype(F32) for part in three_parts(q * (SCALING * LOG2E)))
    first = jnp.where(owner == head, high, 0.0)
    second = jnp.where(
        owner == near,
        roll_lanes(middle, HEAD_DIM),
        jnp.where(owner == far, roll_lanes(low, 2 * HEAD_DIM), 0.0),
    )
    if shift is not None:
        lane = iota((ROWS, LANES), 1) - head * HEAD_DIM
        parts = [part.astype(F32) for part in three_parts(-shift)]
        for at, part in enumerate(parts):
            second = jnp.where(lane == at, part, second)
    return jnp.concatenate([first.astype(BF), second.astype(BF)], axis=1)


def key_side(k, head, owner, shifted):
    near, far = (head + 1) % HEADS_PER_GROUP, (head + 2) % HEADS_PER_GROUP
    second = jnp.where(
        owner == near,
        roll_lanes(k, HEAD_DIM),
        jnp.where(owner == far, roll_lanes(k, 2 * HEAD_DIM), 0.0),
    )
    if shifted:
        lane = iota((ROWS, LANES), 1) - head * HEAD_DIM
        second = jnp.where((lane >= 0) & (lane < 3), 1.0, second)
    return jnp.concatenate([k.astype(BF), second.astype(BF)], axis=1)


def attend_kernel(column_ref, row_ref, q_ref, k_ref, v_ref, mixed_ref, exact_ref, level_ref, bias_s):
    @pl.when(pl.program_id(0) == 0)
    def _():
        write_bias(bias_s, column_ref, row_ref)

    owner = head_of_lane()
    q, k, v = (ref[...].astype(F32) for ref in (q_ref, k_ref, v_ref))
    owner_tile = owner[:TILE]
    for head in range(HEADS_PER_GROUP):
        queries = query_side(q, head, owner)
        keys = key_side(k, head, owner, False)
        values = jnp.concatenate(
            [jnp.where(owner == head, v, 0.0).astype(BF), jnp.ones((ROWS, LANES), BF)], axis=1
        )
        for tile in range(ROWS // TILE):
            rows = slice(tile * TILE, (tile + 1) * TILE)
            scores = dot_nt(queries[rows], keys) + bias_s[rows, :]
            most = jnp.max(scores, axis=-1, keepdims=True)
            raised = jnp.exp2(scores - most).astype(BF)
            both = dot(raised, values)
            total = both[:, LANES:]
            result = both[:, :LANES] / total
            level = most + jnp.log2(total)
            if head == 0:
                exact_ref[rows, :] = result
                level_ref[rows, :] = level
            else:
                mine = owner_tile == head
                exact_ref[rows, :] = jnp.where(mine, result, exact_ref[rows, :])
                level_ref[rows, :] = jnp.where(mine, level, level_ref[rows, :])
    mixed_ref[...] = exact_ref[...].astype(BF)


def group_spec(first=0):
    return pl.BlockSpec((ROWS, LANES), lambda g: (0, first + g))


def whole(shape):
    return pl.BlockSpec(shape, lambda g: (0,) * len(shape))


def attend(segment_column, segment_row, packed):
    return pl.pallas_call(
        attend_kernel,
        grid=(GROUPS,),
        in_specs=[
            whole((ROWS, 1)),
            whole((1, ROWS)),
            group_spec(0),
            group_spec(GROUPS),
            group_spec(2 * GROUPS),
        ],
        out_specs=[group_spec()] * 3,
        out_shape=[
            jax.ShapeDtypeStruct((ROWS, D), BF),
            jax.ShapeDtypeStruct((ROWS, D), F32),
            jax.ShapeDtypeStruct((ROWS, D), F32),
        ],
        scratch_shapes=[pltpu.VMEM((ROWS, ROWS), F32)],
        compiler_params=params(),
        cost_estimate=NO_COST,
        name="attend",
    )(segment_column, segment_row, packed, packed, packed)


def attend_back_kernel(
    column_ref,
    row_ref,
    q_ref,
    k_ref,
    v_ref,
    up_ref,
    exact_ref,
    level_ref,
    out_ref,
    bias_s,
    dqt_s,
    dk_s,
    dv_s,
):
    @pl.when(pl.program_id(0) == 0)
    def _():
        write_bias(bias_s, column_ref, row_ref)

    owner = head_of_lane()
    q, k, v, up = (ref[...].astype(F32) for ref in (q_ref, k_ref, v_ref, up_ref))
    level = level_ref[...]
    keys_t = k.T.astype(BF)
    from_head = iota((LANES, LANES), 0) // HEAD_DIM
    to_head = iota((LANES, LANES), 1) // HEAD_DIM
    spread = ((from_head + 1) % HEADS_PER_GROUP == to_head).astype(F32).astype(BF)
    delta = sum(dot(part, spread) for part in three_parts(up * exact_ref[...]))
    delta_parts = [part.astype(F32) for part in three_parts(-delta)]
    for head in range(HEADS_PER_GROUP):
        mine = owner == head
        near = (head + 1) % HEADS_PER_GROUP
        lane = iota((ROWS, LANES), 1) - near * HEAD_DIM
        queries = query_side(q, head, owner, level)
        keys = key_side(k, head, owner, True)
        up_mine = jnp.where(mine, up, 0.0)
        up_side = up_mine
        for at, part in enumerate(delta_parts):
            up_side = jnp.where(lane == at, part, up_side)
        up_side = up_side.astype(BF)
        up_mine = up_mine.astype(BF)
        value_side = jnp.where((lane >= 0) & (lane < 3), 1.0, v).astype(BF)
        query_mine = jnp.where(mine, q, 0.0).astype(BF)
        head_rows = slice(head * HEAD_DIM, (head + 1) * HEAD_DIM)
        for tile in range(ROWS // TILE):
            rows = slice(tile * TILE, (tile + 1) * TILE)
            weights = jnp.exp2(dot_nt(keys[rows], queries) + bias_s[rows, :])
            pulled = weights * dot_nt(value_side[rows], up_side)
            pulled = pulled.astype(BF)
            dv_part = dot(weights.astype(BF), up_mine)
            dk_part = dot(pulled, query_mine)
            dq_part = dot(keys_t[head_rows, rows], pulled)
            if head == 0:
                dv_s[rows, :] = dv_part
                dk_s[rows, :] = dk_part
            else:
                dv_s[rows, :] += dv_part
                dk_s[rows, :] += dk_part
            if tile == 0:
                dqt_s[head_rows, :] = dq_part
            else:
                dqt_s[head_rows, :] += dq_part
    out_ref[:, :LANES] = (dqt_s[...] * SCALING).T.astype(BF)
    out_ref[:, LANES : 2 * LANES] = (dk_s[...] * SCALING).astype(BF)
    out_ref[:, 2 * LANES :] = dv_s[...].astype(BF)


def attend_back(segment_column, segment_row, packed, upstream, exact, level):
    return pl.pallas_call(
        attend_back_kernel,
        grid=(GROUPS,),
        in_specs=[
            whole((ROWS, 1)),
            whole((1, ROWS)),
            group_spec(0),
            group_spec(GROUPS),
            group_spec(2 * GROUPS),
            group_spec(),
            group_spec(),
            group_spec(),
        ],
        out_specs=pl.BlockSpec((ROWS, 3 * LANES), lambda g: (0, g)),
        out_shape=jax.ShapeDtypeStruct((ROWS, 3 * D), BF),
        scratch_shapes=[
            pltpu.VMEM((ROWS, ROWS), F32),
            pltpu.VMEM((LANES, ROWS), F32),
            pltpu.VMEM((ROWS, LANES), F32),
            pltpu.VMEM((ROWS, LANES), F32),
        ],
        compiler_params=params(),
        cost_estimate=NO_COST,
        name="attend_back",
    )(segment_column, segment_row, packed, packed, packed, upstream, exact, level)


FORWARD_STEP = 512
BACK_STEP = 512


def mlp_kernel(
    ordered_ref,
    mixed_ref,
    w_proj_ref,
    w1_ref,
    w2_ref,
    block_ref,
    middle_ref,
    hidden_ref,
    slope_ref,
    normed_s,
    out_s,
):
    step = pl.program_id(0)

    @pl.when(step == 0)
    def _():
        middle = (
            ordered_ref[...].astype(F32) + dot(mixed_ref[...], w_proj_ref[...])
        ).astype(BF)
        middle_ref[...] = middle
        normed, _ = norm_parts(middle.astype(F32))
        normed_s[...] = normed.astype(BF)
        out_s[...] = middle.astype(F32)

    before = dot(normed_s[...], w1_ref[...])
    half = 0.5 * (1.0 + lax.erf(before * math.sqrt(0.5)))
    density = jnp.exp(before * before * -0.5) * (1.0 / math.sqrt(2.0 * math.pi))
    hidden = (before * half).astype(BF)
    hidden_ref[...] = hidden
    slope_ref[...] = half + before * density
    out_s[...] += dot(hidden, w2_ref[...])

    @pl.when(step == FF // FORWARD_STEP - 1)
    def _():
        block_ref[...] = out_s[...].astype(BF)


def mlp(ordered, mixed, w_proj, w_fc1, w_fc2):
    rows = whole((ROWS, D))
    wide = pl.BlockSpec((ROWS, FORWARD_STEP), lambda i: (0, i))
    return pl.pallas_call(
        mlp_kernel,
        grid=(FF // FORWARD_STEP,),
        in_specs=[
            rows,
            rows,
            whole((D, D)),
            pl.BlockSpec((D, FORWARD_STEP), lambda i: (0, i)),
            pl.BlockSpec((FORWARD_STEP, D), lambda i: (i, 0)),
        ],
        out_specs=[rows, rows, wide, wide],
        out_shape=[
            jax.ShapeDtypeStruct((ROWS, D), BF),
            jax.ShapeDtypeStruct((ROWS, D), BF),
            jax.ShapeDtypeStruct((ROWS, FF), BF),
            jax.ShapeDtypeStruct((ROWS, FF), F32),
        ],
        scratch_shapes=[pltpu.VMEM((ROWS, D), BF), pltpu.VMEM((ROWS, D), F32)],
        compiler_params=params(),
        cost_estimate=NO_COST,
        name="mlp",
    )(ordered, mixed, w_proj, w_fc1, w_fc2)


def mlp_back_kernel(
    up_ref,
    middle_ref,
    slope_ref,
    w_proj_ref,
    w1_ref,
    w2_ref,
    d_middle_ref,
    d_mixed_ref,
    d_before_ref,
    d_normed_s,
):
    step = pl.program_id(0)
    up = up_ref[...]
    d_hidden = dot_nt(up, w2_ref[...]).astype(BF).astype(F32)
    d_before = (d_hidden * slope_ref[...]).astype(BF)
    d_before_ref[...] = d_before
    part = dot_nt(d_before, w1_ref[...])

    @pl.when(step == 0)
    def _():
        d_normed_s[...] = part

    @pl.when(step > 0)
    def _():
        d_normed_s[...] += part

    @pl.when(step == FF // BACK_STEP - 1)
    def _():
        normed, scale = norm_parts(middle_ref[...].astype(F32))
        pulled = norm_pull(normed, scale, d_normed_s[...].astype(BF).astype(F32)).astype(BF)
        d_middle = (up.astype(F32) + pulled.astype(F32)).astype(BF)
        d_middle_ref[...] = d_middle
        d_mixed_ref[...] = dot_nt(d_middle, w_proj_ref[...]).astype(BF)


def mlp_back(upstream, middle, slope, w_proj, w_fc1, w_fc2):
    rows = whole((ROWS, D))
    wide = pl.BlockSpec((ROWS, BACK_STEP), lambda i: (0, i))
    return pl.pallas_call(
        mlp_back_kernel,
        grid=(FF // BACK_STEP,),
        in_specs=[
            rows,
            rows,
            wide,
            whole((D, D)),
            pl.BlockSpec((D, BACK_STEP), lambda i: (0, i)),
            pl.BlockSpec((BACK_STEP, D), lambda i: (i, 0)),
        ],
        out_specs=[rows, rows, wide],
        out_shape=[
            jax.ShapeDtypeStruct((ROWS, D), BF),
            jax.ShapeDtypeStruct((ROWS, D), BF),
            jax.ShapeDtypeStruct((ROWS, FF), BF),
        ],
        scratch_shapes=[pltpu.VMEM((ROWS, D), F32)],
        compiler_params=params(),
        cost_estimate=NO_COST,
        name="mlp_back",
    )(upstream, middle, slope, w_proj, w_fc1, w_fc2)


def group_columns(part, group):
    first = part * D + group * LANES
    return slice(first, first + LANES)


def inputs_back_kernel(ordered_ref, d_packed_ref, d_middle_ref, w_ref, out_ref):
    normed, scale = norm_parts(ordered_ref[...].astype(F32))
    weights = jnp.concatenate(
        [
            w_ref[:, group_columns(part, group)]
            for group in range(GROUPS)
            for part in range(3)
        ],
        axis=1,
    )
    d_normed = dot_nt(d_packed_ref[...], weights)
    pulled = norm_pull(normed, scale, d_normed.astype(BF).astype(F32)).astype(BF)
    out_ref[...] = (d_middle_ref[...].astype(F32) + pulled.astype(F32)).astype(BF)


def inputs_back(ordered, d_packed, d_middle, w_qkv):
    rows = whole((ROWS, D))
    return pl.pallas_call(
        inputs_back_kernel,
        grid=(1,),
        in_specs=[rows, whole((ROWS, 3 * D)), rows, whole((D, 3 * D))],
        out_specs=rows,
        out_shape=jax.ShapeDtypeStruct((ROWS, D), BF),
        compiler_params=params(),
        cost_estimate=NO_COST,
        name="inputs_back",
    )(ordered, d_packed, d_middle, w_qkv)


def transposed(values):
    return values.astype(F32).T.astype(BF)


def weights_back_kernel(
    ordered_ref,
    middle_ref,
    mixed_ref,
    d_middle_ref,
    up_ref,
    d_packed_ref,
    d_before_ref,
    hidden_ref,
    d_w1_ref,
    d_w2_ref,
    rest_ref,
    normed_t_s,
    again_t_s,
    up_t_s,
):
    step = pl.program_id(0)

    @pl.when(step == 0)
    def _():
        normed_t_s[...] = transposed(norm_parts(ordered_ref[...].astype(F32))[0].astype(BF))
        again_t_s[...] = transposed(norm_parts(middle_ref[...].astype(F32))[0].astype(BF))
        up_t_s[...] = transposed(up_ref[...])

    d_w1_ref[...] = dot(again_t_s[...], d_before_ref[...]).astype(BF)
    d_w2_ref[...] = dot(up_t_s[...], hidden_ref[...]).T.astype(BF)

    @pl.when(step < GROUPS)
    def _():
        rest_ref[...] = dot(normed_t_s[...], d_packed_ref[...]).astype(BF)

    @pl.when(step == GROUPS)
    def _():
        rest_ref[...] = dot(transposed(mixed_ref[...]), d_middle_ref[...]).astype(BF)


def weights_back(ordered, middle, mixed, d_middle, upstream, d_packed, d_before, hidden):
    rows = whole((ROWS, D))
    wide = pl.BlockSpec((ROWS, D), lambda i: (0, i))
    down = pl.BlockSpec((D, D), lambda i: (i, 0))
    return pl.pallas_call(
        weights_back_kernel,
        grid=(FF // D,),
        in_specs=[rows] * 5
        + [pl.BlockSpec((ROWS, D), lambda i: (0, jnp.minimum(i, GROUPS - 1))), wide, wide],
        out_specs=[down] * 3,
        out_shape=[jax.ShapeDtypeStruct((FF, D), BF)] * 3,
        scratch_shapes=[pltpu.VMEM((D, ROWS), BF)] * 3,
        compiler_params=params(),
        cost_estimate=NO_COST,
        name="weights_back",
    )(ordered, middle, mixed, d_middle, upstream, d_packed, d_before, hidden)


def place(axis):
    name, stride, size = {
        "y": ("blk", 2, 4),
        "core": ("blk", 1, 2),
        "x": ("sub", 4, 4),
        "z": ("sub", 1, 4),
    }[axis]
    return name, stride, size


def swap(values, axis, kind):
    name, stride, size = place(axis)
    pairs = []
    for index in range(lax.axis_size(name)):
        c = index // stride % size
        partner = 3 - c if kind else c ^ 1
        pairs.append((index, index + (partner - c) * stride))
    return lax.ppermute(values, name, pairs)


def side(axis, kind):
    name, stride, size = place(axis)
    c = lax.axis_index(name) // stride % size
    return c >> 1 if kind else (c ^ (c >> 1)) & 1


def add(a, b):
    return (a.astype(F32) + b.astype(F32)).astype(BF)


def halve_begin(values, axis, kind):
    keep = side(axis, kind)
    half = values.shape[0] // 2
    own = lax.dynamic_slice_in_dim(values, keep * half, half, 0)
    away = lax.dynamic_slice_in_dim(values, (1 - keep) * half, half, 0)
    return own, swap(away, axis, kind)


def halve(values, axis, kind):
    return add(*halve_begin(values, axis, kind))


def meet_begin(values, axis, kind):
    return values, swap(values, axis, kind)


def meet(values, axis, kind):
    return add(*meet_begin(values, axis, kind))


def double(values, axis, kind):
    other = swap(values, axis, kind)
    first = side(axis, kind) == 0
    return jnp.where(
        first, jnp.concatenate([values, other]), jnp.concatenate([other, values])
    )


def spread_again(values, axis):
    for kind in (1, 0):
        values = double(values, axis, kind)
    return values


def finish_kernel(
    keep_ref, w1_ref, w1_other_ref, w2_ref, w2_other_ref, rest_ref, rest_other_ref, qkv_ref, proj_ref, out1_ref, out2_ref
):
    step = pl.program_id(0)
    rows = pl.ds(pl.multiple_of(lax.rem(step, 2) * D, D), D)
    own = step // 2 == keep_ref[0]

    def block(mine_ref, other_ref):
        return jnp.where(own, mine_ref[rows, :].astype(F32), other_ref[rows, :].astype(F32))

    out1_ref[...] = block(w1_ref, w1_other_ref)
    out2_ref[...] = block(w2_ref, w2_other_ref)
    rest = block(rest_ref, rest_other_ref)
    for group in range(GROUPS):

        @pl.when(step == group)
        def _(group=group):
            for part in range(3):
                qkv_ref[:, group_columns(part, group)] = rest[:, part * LANES : (part + 1) * LANES]

    @pl.when(step == GROUPS)
    def _():
        proj_ref[...] = rest


def finish(sums):
    keep = side("core", 0).astype(jnp.int32).reshape(1)
    halves = [part for mine in sums for part in (mine, swap(mine, "core", 0))]
    half = whole((FF // 2, D))
    return pl.pallas_call(
        finish_kernel,
        grid=(FF // D,),
        in_specs=[pl.BlockSpec(memory_space=pltpu.SMEM)] + [half] * 6,
        out_specs=[
            whole((D, 3 * D)),
            whole((D, D)),
            pl.BlockSpec((D, D), lambda i: (0, i)),
            pl.BlockSpec((D, D), lambda i: (i, 0)),
        ],
        out_shape=[
            jax.ShapeDtypeStruct((D, 3 * D), F32),
            jax.ShapeDtypeStruct((D, D), F32),
            jax.ShapeDtypeStruct((D, FF), F32),
            jax.ShapeDtypeStruct((FF, D), F32),
        ],
        compiler_params=params(),
        cost_estimate=NO_COST,
        name="finish",
    )(keep, *halves)


together = lax.optimization_barrier


def exchange(values):
    return lax.all_to_all(values, AXES, split_axis=0, concat_axis=0, tiled=True)


def on_device(points, hilbert_pos, segment_ids, cotangent, w_qkv, w_proj, w_fc1, w_fc2):
    first_lane = ((lax.axis_index(AXES) % 4) * CAP).astype(jnp.int32).reshape(1)
    segment_row = segment_ids.reshape(1, ROWS)
    segment_column = segment_ids.reshape(ROWS, 1)
    wire, slot_row = pack_points(first_lane, hilbert_pos.reshape(1, ROWS), points)
    ordered, packed, landing = land_points(exchange(wire), w_qkv)
    up_received = exchange(pack_rows(slot_row, cotangent))
    mixed, exact, level = attend(segment_column, segment_row, packed)
    block, middle, hidden, slope = mlp(ordered, mixed, w_proj, w_fc1, w_fc2)
    returned, up_received = together((return_rows(landing, block), up_received))
    output_home = exchange(returned)
    upstream = land_rows(landing, up_received)
    d_middle, d_mixed, d_before = mlp_back(upstream, middle, slope, w_proj, w_fc1, w_fc2)
    d_packed = attend_back(segment_column, segment_row, packed, d_mixed, exact, level)
    d_packed, output_home = together((d_packed, output_home))
    back = return_rows(landing, inputs_back(ordered, d_packed, d_middle, w_qkv))
    grad_home = exchange(back)
    d_packed, output_home, _ = together((d_packed, output_home, back))
    sums = weights_back(ordered, middle, mixed, d_middle, upstream, d_packed, d_before, hidden)
    sums = [halve_begin(part, "core", 0) for part in sums]
    output = unpack_rows(slot_row, output_home)
    sums, output, grad_home = together((sums, output, grad_home))
    orders = (("y", "x", "z"), ("x", "z", "y"), ("z", "y", "x"))
    sums = [halve_begin(add(*part), order[0], 0) for part, order in zip(sums, orders)]
    grad_points = unpack_rows(slot_row, grad_home)
    sums, grad_points = together((sums, grad_points))
    sums = [halve(add(*part), order[0], 1) for part, order in zip(sums, orders)]
    for place_in_order in (1, 2):
        for kind in (0, 1):
            sums = [meet(part, order[place_in_order], kind) for part, order in zip(sums, orders)]
    sums = [spread_again(part, order[0]) for part, order in zip(sums, orders)]
    total_qkv, total_proj, total_w1, total_w2 = finish(sums)
    return output, grad_points, total_qkv, total_proj, total_w1, total_w2


def solution(mesh):
    placed = (P(AXES, None), P(AXES), P(AXES), P(AXES, None), P(), P(), P(), P())
    return jax.shard_map(
        on_device,
        mesh=mesh,
        in_specs=placed,
        out_specs=(P(AXES, None), P(AXES, None), P(), P(), P(), P()),
        check_vma=False,
    )
```

```python
import math

import jax
import jax.numpy as jnp
from jax import lax
from jax.experimental import pallas as pl
from jax.experimental.pallas import tpu as pltpu
from jax.sharding import PartitionSpec as P

AXES = ("blk", "sub")
ROWS = 1024
D = 384
FF = 1536
LANES = 128
HEAD_DIM = 32
GROUPS = D // LANES
HEADS_PER_GROUP = LANES // HEAD_DIM
SHARDS = 128
CAP = 32
SLOTS = SHARDS * CAP
STEP_SHARDS = 64
STEP_SLOTS = STEP_SHARDS * CAP
STEPS = SHARDS // STEP_SHARDS
WIRE_ROWS = 3 * CAP + 2
EPSILON = 1e-05
SCALING = 1.0 / math.sqrt(HEAD_DIM)
LOG2E = 1.4426950408889634
MASKED = -1e30
TILE = 256
BF = jnp.bfloat16
F32 = jnp.float32

NO_COST = pl.CostEstimate(flops=1, bytes_accessed=1, transcendentals=0)

NT = (((1,), (1,)), ((), ()))


def dot(a, b):
    return jnp.dot(a, b, preferred_element_type=F32)


def dot_nt(a, b):
    return lax.dot_general(a, b, NT, preferred_element_type=F32)


def iota(shape, axis):
    return lax.broadcasted_iota(jnp.int32, shape, axis)


def params(grid_dims=1, mib=56):
    return pltpu.CompilerParams(
        vmem_limit_bytes=mib * 1024 * 1024,
        dimension_semantics=("arbitrary",) * grid_dims,
    )


def row_to_column(row):
    return jnp.broadcast_to(row, (8, row.shape[1])).T[:, 0:1]


def one_hot_slots(slot_row, first):
    ids = iota((STEP_SLOTS, ROWS), 0) + first
    return (ids == slot_row).astype(F32).astype(BF)


def pack_points_kernel(lane_ref, pos_ref, x_ref, out_ref, slot_ref, high_s, low_s):
    step = pl.program_id(0)

    @pl.when(step == 0)
    def _():
        pos = pos_ref[...]
        target = pos >> 10
        offset = pos & (ROWS - 1)
        member = iota((SHARDS, ROWS), 0) == target
        member_bf = member.astype(F32).astype(BF)
        before = (iota((ROWS, ROWS), 0) < iota((ROWS, ROWS), 1)).astype(F32).astype(BF)
        earlier = dot(member_bf, before)
        rank = jnp.sum(jnp.where(member, earlier, 0.0), axis=0, keepdims=True).astype(jnp.int32)
        slot_ref[...] = target * CAP + rank
        lane = (iota((LANES, ROWS), 0) == rank + lane_ref[0]).astype(F32).astype(BF)
        high = ((offset >> 5) + 1).astype(F32)
        low = (offset & 31).astype(F32)
        high_s[...] = dot_nt(jnp.where(member, high, 0.0).astype(BF), lane)
        low_s[...] = dot_nt(jnp.where(member, low, 0.0).astype(BF), lane)

    picked = dot(one_hot_slots(slot_ref[...], step * STEP_SLOTS), x_ref[...]).astype(BF)
    for piece in range(3):
        out_ref[:, piece * CAP : (piece + 1) * CAP, :] = picked[
            :, piece * LANES : (piece + 1) * LANES
        ].reshape(STEP_SHARDS, CAP, LANES)
    first = pl.multiple_of(step * STEP_SHARDS, STEP_SHARDS)
    high = high_s[pl.ds(first, STEP_SHARDS), :]
    low = low_s[pl.ds(first, STEP_SHARDS), :]
    for s in range(STEP_SHARDS):
        pair = jnp.concatenate([high[s : s + 1], low[s : s + 1]], axis=0)
        out_ref[s, 3 * CAP : WIRE_ROWS, :] = pair.astype(BF)


def pack_points(first_lane, pos_row, points):
    return pl.pallas_call(
        pack_points_kernel,
        grid=(STEPS,),
        in_specs=[
            pl.BlockSpec(memory_space=pltpu.SMEM),
            pl.BlockSpec((1, ROWS), lambda i: (0, 0)),
            pl.BlockSpec((ROWS, D), lambda i: (0, 0)),
        ],
        out_specs=[
            pl.BlockSpec((STEP_SHARDS, WIRE_ROWS, LANES), lambda i: (i, 0, 0)),
            pl.BlockSpec((1, ROWS), lambda i: (0, 0)),
        ],
        out_shape=[
            jax.ShapeDtypeStruct((SHARDS, WIRE_ROWS, LANES), BF),
            jax.ShapeDtypeStruct((1, ROWS), jnp.int32),
        ],
        scratch_shapes=[pltpu.VMEM((SHARDS, LANES), F32), pltpu.VMEM((SHARDS, LANES), F32)],
        compiler_params=params(),
        cost_estimate=NO_COST,
        name="pack_points",
    )(first_lane, pos_row, points)


def pack_rows_kernel(slot_ref, x_ref, out_ref):
    picked = dot(one_hot_slots(slot_ref[...], pl.program_id(0) * STEP_SLOTS), x_ref[...])
    out_ref[...] = picked.astype(BF).reshape(STEP_SHARDS, CAP, D)


def pack_rows(slot_row, values):
    return pl.pallas_call(
        pack_rows_kernel,
        grid=(STEPS,),
        in_specs=[
            pl.BlockSpec((1, ROWS), lambda i: (0, 0)),
            pl.BlockSpec((ROWS, D), lambda i: (0, 0)),
        ],
        out_specs=pl.BlockSpec((STEP_SHARDS, CAP, D), lambda i: (i, 0, 0)),
        out_shape=jax.ShapeDtypeStruct((SHARDS, CAP, D), BF),
        compiler_params=params(),
        cost_estimate=NO_COST,
        name="pack_rows",
    )(slot_row, values)


def unpack_rows_kernel(slot_ref, home_ref, out_ref, column_s, total_s):
    step = pl.program_id(0)

    @pl.when(step == 0)
    def _():
        column_s[...] = jnp.broadcast_to(
            row_to_column(slot_ref[...].astype(F32)).astype(jnp.int32), (ROWS, LANES)
        )
        total_s[...] = jnp.zeros_like(total_s)

    wide = jnp.concatenate([column_s[...]] * (STEP_SLOTS // LANES), axis=1)
    hot = (iota((ROWS, STEP_SLOTS), 1) + step * STEP_SLOTS == wide).astype(F32).astype(BF)
    total_s[...] += dot(hot, home_ref[...].reshape(STEP_SLOTS, D))

    @pl.when(step == STEPS - 1)
    def _():
        out_ref[...] = total_s[...].astype(BF)


def unpack_rows(slot_row, home):
    return pl.pallas_call(
        unpack_rows_kernel,
        grid=(STEPS,),
        in_specs=[
            pl.BlockSpec((1, ROWS), lambda i: (0, 0)),
            pl.BlockSpec((STEP_SHARDS, CAP, D), lambda i: (i, 0, 0)),
        ],
        out_specs=pl.BlockSpec((ROWS, D), lambda i: (0, 0)),
        out_shape=jax.ShapeDtypeStruct((ROWS, D), BF),
        scratch_shapes=[pltpu.VMEM((ROWS, LANES), jnp.int32), pltpu.VMEM((ROWS, D), F32)],
        compiler_params=params(),
        cost_estimate=NO_COST,
        name="unpack_rows",
    )(slot_row, home)


def norm_parts(values):
    centred = values - jnp.mean(values, axis=-1, keepdims=True)
    spread = jnp.mean(centred * centred, axis=-1, keepdims=True)
    scale = lax.rsqrt(spread + EPSILON)
    return centred * scale, scale


def norm_pull(normed, scale, upstream):
    across = jnp.mean(upstream, axis=-1, keepdims=True)
    along = jnp.mean(upstream * normed, axis=-1, keepdims=True)
    return scale * (upstream - across - normed * along)


def landing_one_hot(landing):
    return (iota((ROWS, STEP_SLOTS), 0) == landing).astype(F32).astype(BF)


def land_points_kernel(recv_ref, w_ref, ordered_ref, packed_ref, landing_ref, total_s):
    step = pl.program_id(0)

    @pl.when(step == 0)
    def _():
        total_s[...] = jnp.zeros_like(total_s)

    pieces = []
    for group in range(STEP_SHARDS // 4):
        pair = recv_ref[4 * group, 3 * CAP : WIRE_ROWS, :].astype(F32)
        for other in range(1, 4):
            pair = pair + recv_ref[4 * group + other, 3 * CAP : WIRE_ROWS, :].astype(F32)
        pieces.append((pair[0:1] - 1.0) * 32.0 + pair[1:2])
    landing = jnp.concatenate(pieces, axis=1).astype(jnp.int32)
    landing_ref[0] = landing
    rows = jnp.concatenate(
        [
            recv_ref[:, piece * CAP : (piece + 1) * CAP, :].reshape(STEP_SLOTS, LANES)
            for piece in range(3)
        ],
        axis=1,
    )
    total_s[...] += dot(landing_one_hot(landing), rows)

    @pl.when(step == STEPS - 1)
    def _():
        ordered = total_s[...]
        ordered_ref[...] = ordered.astype(BF)
        normed, _ = norm_parts(ordered)
        packed_ref[...] = dot(normed.astype(BF), w_ref[...]).astype(BF)


def land_points(received, w_qkv):
    return pl.pallas_call(
        land_points_kernel,
        grid=(STEPS,),
        in_specs=[
            pl.BlockSpec((STEP_SHARDS, WIRE_ROWS, LANES), lambda i: (i, 0, 0)),
            pl.BlockSpec((D, 3 * D), lambda i: (0, 0)),
        ],
        out_specs=[
            pl.BlockSpec((ROWS, D), lambda i: (0, 0)),
            pl.BlockSpec((ROWS, 3 * D), lambda i: (0, 0)),
            pl.BlockSpec((1, 1, STEP_SLOTS), lambda i: (i, 0, 0)),
        ],
        out_shape=[
            jax.ShapeDtypeStruct((ROWS, D), BF),
            jax.ShapeDtypeStruct((ROWS, 3 * D), BF),
            jax.ShapeDtypeStruct((STEPS, 1, STEP_SLOTS), jnp.int32),
        ],
        scratch_shapes=[pltpu.VMEM((ROWS, D), F32)],
        compiler_params=params(),
        cost_estimate=NO_COST,
        name="land_points",
    )(received, w_qkv)


def land_rows_kernel(landing_ref, recv_ref, out_ref, total_s):
    step = pl.program_id(0)

    @pl.when(step == 0)
    def _():
        total_s[...] = jnp.zeros_like(total_s)

    total_s[...] += dot(landing_one_hot(landing_ref[0]), recv_ref[...].reshape(STEP_SLOTS, D))

    @pl.when(step == STEPS - 1)
    def _():
        out_ref[...] = total_s[...].astype(BF)


def land_rows(landing, received):
    return pl.pallas_call(
        land_rows_kernel,
        grid=(STEPS,),
        in_specs=[
            pl.BlockSpec((1, 1, STEP_SLOTS), lambda i: (i, 0, 0)),
            pl.BlockSpec((STEP_SHARDS, CAP, D), lambda i: (i, 0, 0)),
        ],
        out_specs=pl.BlockSpec((ROWS, D), lambda i: (0, 0)),
        out_shape=jax.ShapeDtypeStruct((ROWS, D), BF),
        scratch_shapes=[pltpu.VMEM((ROWS, D), F32)],
        compiler_params=params(),
        cost_estimate=NO_COST,
        name="land_rows",
    )(landing, received)


def return_one_hot(landing):
    column = row_to_column(landing.astype(F32)).astype(jnp.int32)
    return (iota((STEP_SLOTS, ROWS), 1) == column).astype(F32).astype(BF)


def return_rows_kernel(landing_ref, x_ref, out_ref):
    picked = dot(return_one_hot(landing_ref[0]), x_ref[...])
    out_ref[...] = picked.astype(BF).reshape(STEP_SHARDS, CAP, D)


def return_rows(landing, values):
    return pl.pallas_call(
        return_rows_kernel,
        grid=(STEPS,),
        in_specs=[
            pl.BlockSpec((1, 1, STEP_SLOTS), lambda i: (i, 0, 0)),
            pl.BlockSpec((ROWS, D), lambda i: (0, 0)),
        ],
        out_specs=pl.BlockSpec((STEP_SHARDS, CAP, D), lambda i: (i, 0, 0)),
        out_shape=jax.ShapeDtypeStruct((SHARDS, CAP, D), BF),
        compiler_params=params(),
        cost_estimate=NO_COST,
        name="return_rows",
    )(landing, values)


def three_parts(values):
    high = values.astype(BF)
    rest = values - high.astype(F32)
    middle = rest.astype(BF)
    return high, middle, (rest - middle.astype(F32)).astype(BF)


def write_bias(bias_s, column_ref, row_ref):
    bias_s[...] = jnp.where(column_ref[...] == row_ref[...], 0.0, MASKED)


def head_of_lane():
    return iota((ROWS, LANES), 1) // HEAD_DIM


def roll_lanes(values, by):
    return pltpu.roll(values.astype(F32), by % LANES, 1)


def query_side(q, head, owner, shift=None):
    near, far = (head + 1) % HEADS_PER_GROUP, (head + 2) % HEADS_PER_GROUP
    high, middle, low = (part.astype(F32) for part in three_parts(q * (SCALING * LOG2E)))
    side = jnp.where(
        owner == head,
        high,
        jnp.where(
            owner == near,
            roll_lanes(middle, HEAD_DIM),
            jnp.where(owner == far, roll_lanes(low, 2 * HEAD_DIM), 0.0),
        ),
    )
    if shift is not None:
        last = (head + 3) % HEADS_PER_GROUP
        lane = iota((ROWS, LANES), 1) - last * HEAD_DIM
        shift = roll_lanes(shift, 3 * HEAD_DIM)
        for at, part in enumerate(three_parts(-shift)):
            side = jnp.where(lane == at, part.astype(F32), side)
    return side.astype(BF)


def key_side(k, head, owner, shifted):
    near, far = (head + 1) % HEADS_PER_GROUP, (head + 2) % HEADS_PER_GROUP
    side = jnp.where(
        owner == head,
        k,
        jnp.where(
            owner == near,
            roll_lanes(k, HEAD_DIM),
            jnp.where(owner == far, roll_lanes(k, 2 * HEAD_DIM), 0.0),
        ),
    )
    if shifted:
        last = (head + 3) % HEADS_PER_GROUP
        lane = iota((ROWS, LANES), 1) - last * HEAD_DIM
        side = jnp.where((lane >= 0) & (lane < 3), 1.0, side)
    return side.astype(BF)


def attend_kernel(column_ref, row_ref, q_ref, k_ref, v_ref, mixed_ref, exact_ref, level_ref, bias_s):
    @pl.when(pl.program_id(0) == 0)
    def _():
        write_bias(bias_s, column_ref, row_ref)

    owner = head_of_lane()
    q, k, v = (ref[...].astype(F32) for ref in (q_ref, k_ref, v_ref))
    owner_tile = owner[:TILE]
    for head in range(HEADS_PER_GROUP):
        queries = query_side(q, head, owner)
        keys = key_side(k, head, owner, False)
        values = jnp.concatenate(
            [jnp.where(owner == head, v, 0.0).astype(BF), jnp.ones((ROWS, LANES), BF)], axis=1
        )
        for tile in range(ROWS // TILE):
            rows = slice(tile * TILE, (tile + 1) * TILE)
            scores = dot_nt(queries[rows], keys) + bias_s[rows, :]
            most = jnp.max(scores, axis=-1, keepdims=True)
            raised = jnp.exp2(scores - most).astype(BF)
            both = dot(raised, values)
            total = both[:, LANES:]
            result = both[:, :LANES] / total
            level = most + jnp.log2(total)
            if head == 0:
                exact_ref[rows, :] = result
                level_ref[rows, :] = level
            else:
                mine = owner_tile == head
                exact_ref[rows, :] = jnp.where(mine, result, exact_ref[rows, :])
                level_ref[rows, :] = jnp.where(mine, level, level_ref[rows, :])
    mixed_ref[...] = exact_ref[...].astype(BF)


def group_spec(first=0):
    return pl.BlockSpec((ROWS, LANES), lambda g: (0, first + g))


def whole(shape):
    return pl.BlockSpec(shape, lambda g: (0,) * len(shape))


def attend(segment_column, segment_row, packed):
    return pl.pallas_call(
        attend_kernel,
        grid=(GROUPS,),
        in_specs=[
            whole((ROWS, 1)),
            whole((1, ROWS)),
            group_spec(0),
            group_spec(GROUPS),
            group_spec(2 * GROUPS),
        ],
        out_specs=[group_spec()] * 3,
        out_shape=[
            jax.ShapeDtypeStruct((ROWS, D), BF),
            jax.ShapeDtypeStruct((ROWS, D), F32),
            jax.ShapeDtypeStruct((ROWS, D), F32),
        ],
        scratch_shapes=[pltpu.VMEM((ROWS, ROWS), F32)],
        compiler_params=params(),
        cost_estimate=NO_COST,
        name="attend",
    )(segment_column, segment_row, packed, packed, packed)


def attend_back_kernel(
    column_ref,
    row_ref,
    q_ref,
    k_ref,
    v_ref,
    up_ref,
    exact_ref,
    level_ref,
    out_ref,
    bias_s,
    dqt_s,
    dk_s,
    dv_s,
):
    @pl.when(pl.program_id(0) == 0)
    def _():
        write_bias(bias_s, column_ref, row_ref)

    owner = head_of_lane()
    q, k, v, up = (ref[...].astype(F32) for ref in (q_ref, k_ref, v_ref, up_ref))
    level = level_ref[...]
    keys_t = k.T.astype(BF)
    from_head = iota((LANES, LANES), 0) // HEAD_DIM
    to_head = iota((LANES, LANES), 1) // HEAD_DIM
    spread = ((from_head + 1) % HEADS_PER_GROUP == to_head).astype(F32).astype(BF)
    delta = sum(dot(part, spread) for part in three_parts(up * exact_ref[...]))
    delta_parts = [part.astype(F32) for part in three_parts(-delta)]
    for head in range(HEADS_PER_GROUP):
        mine = owner == head
        near = (head + 1) % HEADS_PER_GROUP
        lane = iota((ROWS, LANES), 1) - near * HEAD_DIM
        queries = query_side(q, head, owner, level)
        keys = key_side(k, head, owner, True)
        up_mine = jnp.where(mine, up, 0.0)
        up_side = up_mine
        for at, part in enumerate(delta_parts):
            up_side = jnp.where(lane == at, part, up_side)
        up_side = up_side.astype(BF)
        up_mine = up_mine.astype(BF)
        value_side = jnp.where((lane >= 0) & (lane < 3), 1.0, v).astype(BF)
        query_mine = jnp.where(mine, q, 0.0).astype(BF)
        head_rows = slice(head * HEAD_DIM, (head + 1) * HEAD_DIM)
        dv_part = dk_part = 0.0
        for tile in range(ROWS // TILE):
            at = slice(tile * TILE, (tile + 1) * TILE)
            weights = jnp.exp2(dot_nt(keys, queries[at]) + bias_s[:, at])
            pulled = (weights * dot_nt(value_side, up_side[at])).astype(BF)
            dv_part = dv_part + dot(weights.astype(BF), up_mine[at])
            dk_part = dk_part + dot(pulled, query_mine[at])
            dqt_s[head_rows, at] = dot(keys_t[head_rows], pulled)
        if head == 0:
            dv_s[...] = dv_part
            dk_s[...] = dk_part
        else:
            dv_s[...] += dv_part
            dk_s[...] += dk_part
    out_ref[:, :LANES] = (dqt_s[...] * SCALING).T.astype(BF)
    out_ref[:, LANES : 2 * LANES] = (dk_s[...] * SCALING).astype(BF)
    out_ref[:, 2 * LANES :] = dv_s[...].astype(BF)


def attend_back(segment_column, segment_row, packed, upstream, exact, level):
    return pl.pallas_call(
        attend_back_kernel,
        grid=(GROUPS,),
        in_specs=[
            whole((ROWS, 1)),
            whole((1, ROWS)),
            group_spec(0),
            group_spec(GROUPS),
            group_spec(2 * GROUPS),
            group_spec(),
            group_spec(),
            group_spec(),
        ],
        out_specs=pl.BlockSpec((ROWS, 3 * LANES), lambda g: (0, g)),
        out_shape=jax.ShapeDtypeStruct((ROWS, 3 * D), BF),
        scratch_shapes=[
            pltpu.VMEM((ROWS, ROWS), F32),
            pltpu.VMEM((LANES, ROWS), F32),
            pltpu.VMEM((ROWS, LANES), F32),
            pltpu.VMEM((ROWS, LANES), F32),
        ],
        compiler_params=params(),
        cost_estimate=NO_COST,
        name="attend_back",
    )(segment_column, segment_row, packed, packed, packed, upstream, exact, level)


FORWARD_STEP = 512
BACK_STEP = 512


def mlp_kernel(
    ordered_ref,
    mixed_ref,
    w_proj_ref,
    w1_ref,
    w2_ref,
    block_ref,
    middle_ref,
    hidden_ref,
    slope_ref,
    normed_s,
    out_s,
):
    step = pl.program_id(0)

    @pl.when(step == 0)
    def _():
        middle = (
            ordered_ref[...].astype(F32) + dot(mixed_ref[...], w_proj_ref[...])
        ).astype(BF)
        middle_ref[...] = middle
        normed, _ = norm_parts(middle.astype(F32))
        normed_s[...] = normed.astype(BF)
        out_s[...] = middle.astype(F32)

    before = dot(normed_s[...], w1_ref[...])
    half = 0.5 * (1.0 + lax.erf(before * math.sqrt(0.5)))
    density = jnp.exp(before * before * -0.5) * (1.0 / math.sqrt(2.0 * math.pi))
    hidden = (before * half).astype(BF)
    hidden_ref[...] = hidden
    slope_ref[...] = half + before * density
    out_s[...] += dot(hidden, w2_ref[...])

    @pl.when(step == FF // FORWARD_STEP - 1)
    def _():
        block_ref[...] = out_s[...].astype(BF)


def mlp(ordered, mixed, w_proj, w_fc1, w_fc2):
    rows = whole((ROWS, D))
    wide = pl.BlockSpec((ROWS, FORWARD_STEP), lambda i: (0, i))
    return pl.pallas_call(
        mlp_kernel,
        grid=(FF // FORWARD_STEP,),
        in_specs=[
            rows,
            rows,
            whole((D, D)),
            pl.BlockSpec((D, FORWARD_STEP), lambda i: (0, i)),
            pl.BlockSpec((FORWARD_STEP, D), lambda i: (i, 0)),
        ],
        out_specs=[rows, rows, wide, wide],
        out_shape=[
            jax.ShapeDtypeStruct((ROWS, D), BF),
            jax.ShapeDtypeStruct((ROWS, D), BF),
            jax.ShapeDtypeStruct((ROWS, FF), BF),
            jax.ShapeDtypeStruct((ROWS, FF), F32),
        ],
        scratch_shapes=[pltpu.VMEM((ROWS, D), BF), pltpu.VMEM((ROWS, D), F32)],
        compiler_params=params(),
        cost_estimate=NO_COST,
        name="mlp",
    )(ordered, mixed, w_proj, w_fc1, w_fc2)


def mlp_back_kernel(
    up_ref,
    middle_ref,
    slope_ref,
    w_proj_ref,
    w1_ref,
    w2_ref,
    d_middle_ref,
    d_mixed_ref,
    d_before_ref,
    d_normed_s,
):
    step = pl.program_id(0)
    up = up_ref[...]
    d_hidden = dot_nt(up, w2_ref[...]).astype(BF).astype(F32)
    d_before = (d_hidden * slope_ref[...]).astype(BF)
    d_before_ref[...] = d_before
    part = dot_nt(d_before, w1_ref[...])

    @pl.when(step == 0)
    def _():
        d_normed_s[...] = part

    @pl.when(step > 0)
    def _():
        d_normed_s[...] += part

    @pl.when(step == FF // BACK_STEP - 1)
    def _():
        normed, scale = norm_parts(middle_ref[...].astype(F32))
        pulled = norm_pull(normed, scale, d_normed_s[...].astype(BF).astype(F32)).astype(BF)
        d_middle = (up.astype(F32) + pulled.astype(F32)).astype(BF)
        d_middle_ref[...] = d_middle
        d_mixed_ref[...] = dot_nt(d_middle, w_proj_ref[...]).astype(BF)


def mlp_back(upstream, middle, slope, w_proj, w_fc1, w_fc2):
    rows = whole((ROWS, D))
    wide = pl.BlockSpec((ROWS, BACK_STEP), lambda i: (0, i))
    return pl.pallas_call(
        mlp_back_kernel,
        grid=(FF // BACK_STEP,),
        in_specs=[
            rows,
            rows,
            wide,
            whole((D, D)),
            pl.BlockSpec((D, BACK_STEP), lambda i: (0, i)),
            pl.BlockSpec((BACK_STEP, D), lambda i: (i, 0)),
        ],
        out_specs=[rows, rows, wide],
        out_shape=[
            jax.ShapeDtypeStruct((ROWS, D), BF),
            jax.ShapeDtypeStruct((ROWS, D), BF),
            jax.ShapeDtypeStruct((ROWS, FF), BF),
        ],
        scratch_shapes=[pltpu.VMEM((ROWS, D), F32)],
        compiler_params=params(),
        cost_estimate=NO_COST,
        name="mlp_back",
    )(upstream, middle, slope, w_proj, w_fc1, w_fc2)


def group_columns(part, group):
    first = part * D + group * LANES
    return slice(first, first + LANES)


def inputs_back_kernel(
    landing_ref, ordered_ref, d_packed_ref, d_middle_ref, w_ref, out_ref, d_inputs_s
):
    @pl.when(pl.program_id(0) == 0)
    def _():
        normed, scale = norm_parts(ordered_ref[...].astype(F32))
        weights = jnp.concatenate(
            [
                w_ref[:, group_columns(part, group)]
                for group in range(GROUPS)
                for part in range(3)
            ],
            axis=1,
        )
        d_normed = dot_nt(d_packed_ref[...], weights)
        pulled = norm_pull(normed, scale, d_normed.astype(BF).astype(F32)).astype(BF)
        d_inputs_s[...] = (d_middle_ref[...].astype(F32) + pulled.astype(F32)).astype(BF)

    picked = dot(return_one_hot(landing_ref[0]), d_inputs_s[...])
    out_ref[...] = picked.astype(BF).reshape(STEP_SHARDS, CAP, D)


def inputs_back(landing, ordered, d_packed, d_middle, w_qkv):
    rows = whole((ROWS, D))
    return pl.pallas_call(
        inputs_back_kernel,
        grid=(STEPS,),
        in_specs=[
            pl.BlockSpec((1, 1, STEP_SLOTS), lambda i: (i, 0, 0)),
            rows,
            whole((ROWS, 3 * D)),
            rows,
            whole((D, 3 * D)),
        ],
        out_specs=pl.BlockSpec((STEP_SHARDS, CAP, D), lambda i: (i, 0, 0)),
        out_shape=jax.ShapeDtypeStruct((SHARDS, CAP, D), BF),
        scratch_shapes=[pltpu.VMEM((ROWS, D), BF)],
        compiler_params=params(),
        cost_estimate=NO_COST,
        name="inputs_back",
    )(landing, ordered, d_packed, d_middle, w_qkv)


def transposed(values):
    return values.astype(F32).T.astype(BF)


def weights_back_kernel(
    ordered_ref,
    middle_ref,
    mixed_ref,
    d_middle_ref,
    up_ref,
    d_packed_ref,
    d_before_ref,
    hidden_ref,
    d_w1_ref,
    d_w2_ref,
    rest_ref,
    normed_t_s,
    again_t_s,
    up_t_s,
):
    step = pl.program_id(0)

    @pl.when(step == 0)
    def _():
        normed_t_s[...] = transposed(norm_parts(ordered_ref[...].astype(F32))[0].astype(BF))
        again_t_s[...] = transposed(norm_parts(middle_ref[...].astype(F32))[0].astype(BF))
        up_t_s[...] = transposed(up_ref[...])

    d_w1_ref[...] = dot(again_t_s[...], d_before_ref[...]).astype(BF)
    d_w2_ref[...] = dot(up_t_s[...], hidden_ref[...]).T.astype(BF)

    @pl.when(step < GROUPS)
    def _():
        rest_ref[...] = dot(normed_t_s[...], d_packed_ref[...]).astype(BF)

    @pl.when(step == GROUPS)
    def _():
        rest_ref[...] = dot(transposed(mixed_ref[...]), d_middle_ref[...]).astype(BF)


def weights_back(ordered, middle, mixed, d_middle, upstream, d_packed, d_before, hidden):
    rows = whole((ROWS, D))
    wide = pl.BlockSpec((ROWS, D), lambda i: (0, i))
    down = pl.BlockSpec((D, D), lambda i: (i, 0))
    return pl.pallas_call(
        weights_back_kernel,
        grid=(FF // D,),
        in_specs=[rows] * 5
        + [pl.BlockSpec((ROWS, D), lambda i: (0, jnp.minimum(i, GROUPS - 1))), wide, wide],
        out_specs=[down] * 3,
        out_shape=[jax.ShapeDtypeStruct((FF, D), BF)] * 3,
        scratch_shapes=[pltpu.VMEM((D, ROWS), BF)] * 3,
        compiler_params=params(),
        cost_estimate=NO_COST,
        name="weights_back",
    )(ordered, middle, mixed, d_middle, upstream, d_packed, d_before, hidden)


def place(axis):
    name, stride, size = {
        "y": ("blk", 2, 4),
        "core": ("blk", 1, 2),
        "x": ("sub", 4, 4),
        "z": ("sub", 1, 4),
    }[axis]
    return name, stride, size


def swap(values, axis, kind):
    name, stride, size = place(axis)
    pairs = []
    for index in range(lax.axis_size(name)):
        c = index // stride % size
        partner = 3 - c if kind else c ^ 1
        pairs.append((index, index + (partner - c) * stride))
    return lax.ppermute(values, name, pairs)


def side(axis, kind):
    name, stride, size = place(axis)
    c = lax.axis_index(name) // stride % size
    return c >> 1 if kind else (c ^ (c >> 1)) & 1


def add(a, b):
    return (a.astype(F32) + b.astype(F32)).astype(BF)


def halve_begin(values, axis, kind):
    keep = side(axis, kind)
    half = values.shape[0] // 2
    own = lax.dynamic_slice_in_dim(values, keep * half, half, 0)
    away = lax.dynamic_slice_in_dim(values, (1 - keep) * half, half, 0)
    return own, swap(away, axis, kind)


def halve(values, axis, kind):
    return add(*halve_begin(values, axis, kind))


def meet_begin(values, axis, kind):
    return values, swap(values, axis, kind)


def meet(values, axis, kind):
    return add(*meet_begin(values, axis, kind))


def double(values, axis, kind):
    other = swap(values, axis, kind)
    first = side(axis, kind) == 0
    return jnp.where(
        first, jnp.concatenate([values, other]), jnp.concatenate([other, values])
    )


def spread_again(values, axis):
    for kind in (1, 0):
        values = double(values, axis, kind)
    return values


def finish_kernel(
    keep_ref, w1_ref, w1_other_ref, w2_ref, w2_other_ref, rest_ref, rest_other_ref, qkv_ref, proj_ref, out1_ref, out2_ref
):
    step = pl.program_id(0)
    own = step // 2 == keep_ref[0]

    def block(mine_ref, other_ref):
        return jnp.where(own, mine_ref[...].astype(F32), other_ref[...].astype(F32))

    out1_ref[...] = block(w1_ref, w1_other_ref)
    out2_ref[...] = block(w2_ref, w2_other_ref)
    rest = block(rest_ref, rest_other_ref)
    for group in range(GROUPS):

        @pl.when(step == group)
        def _(group=group):
            for part in range(3):
                qkv_ref[:, group_columns(part, group)] = rest[:, part * LANES : (part + 1) * LANES]

    @pl.when(step == GROUPS)
    def _():
        proj_ref[...] = rest


def finish(sums):
    keep = side("core", 0).astype(jnp.int32).reshape(1)
    halves = [part for mine in sums for part in (mine, swap(mine, "core", 0))]
    half = pl.BlockSpec((D, D), lambda i: (i % 2, 0))
    return pl.pallas_call(
        finish_kernel,
        grid=(FF // D,),
        in_specs=[pl.BlockSpec(memory_space=pltpu.SMEM)] + [half] * 6,
        out_specs=[
            whole((D, 3 * D)),
            whole((D, D)),
            pl.BlockSpec((D, D), lambda i: (0, i)),
            pl.BlockSpec((D, D), lambda i: (i, 0)),
        ],
        out_shape=[
            jax.ShapeDtypeStruct((D, 3 * D), F32),
            jax.ShapeDtypeStruct((D, D), F32),
            jax.ShapeDtypeStruct((D, FF), F32),
            jax.ShapeDtypeStruct((FF, D), F32),
        ],
        compiler_params=params(),
        cost_estimate=NO_COST,
        name="finish",
    )(keep, *halves)


together = lax.optimization_barrier


def exchange(values):
    return lax.all_to_all(values, AXES, split_axis=0, concat_axis=0, tiled=True)


def on_device(points, hilbert_pos, segment_ids, cotangent, w_qkv, w_proj, w_fc1, w_fc2):
    first_lane = ((lax.axis_index(AXES) % 4) * CAP).astype(jnp.int32).reshape(1)
    segment_row = segment_ids.reshape(1, ROWS)
    segment_column = segment_ids.reshape(ROWS, 1)
    wire, slot_row = pack_points(first_lane, hilbert_pos.reshape(1, ROWS), points)
    ordered, packed, landing = land_points(exchange(wire), w_qkv)
    up_slots, segment_column = together((pack_rows(slot_row, cotangent), segment_column))
    up_received = exchange(up_slots)
    mixed, exact, level = attend(segment_column, segment_row, packed)
    block, middle, hidden, slope = mlp(ordered, mixed, w_proj, w_fc1, w_fc2)
    returned, up_received = together((return_rows(landing, block), up_received))
    output_home = exchange(returned)
    upstream = land_rows(landing, up_received)
    d_middle, d_mixed, d_before = mlp_back(upstream, middle, slope, w_proj, w_fc1, w_fc2)
    d_packed = attend_back(segment_column, segment_row, packed, d_mixed, exact, level)
    d_packed, output_home = together((d_packed, output_home))
    back = inputs_back(landing, ordered, d_packed, d_middle, w_qkv)
    grad_home = exchange(back)
    d_packed, output_home, _ = together((d_packed, output_home, back))
    sums = weights_back(ordered, middle, mixed, d_middle, upstream, d_packed, d_before, hidden)
    sums = [halve_begin(part, "core", 0) for part in sums]
    output = unpack_rows(slot_row, output_home)
    sums, output, grad_home = together((sums, output, grad_home))
    orders = (("y", "x", "z"), ("x", "z", "y"), ("z", "y", "x"))
    sums = [halve_begin(add(*part), order[0], 0) for part, order in zip(sums, orders)]
    grad_points = unpack_rows(slot_row, grad_home)
    sums, grad_points = together((sums, grad_points))
    sums = [halve(add(*part), order[0], 1) for part, order in zip(sums, orders)]
    for place_in_order in (1, 2):
        for kind in (0, 1):
            sums = [meet(part, order[place_in_order], kind) for part, order in zip(sums, orders)]
    sums = [spread_again(part, order[0]) for part, order in zip(sums, orders)]
    total_qkv, total_proj, total_w1, total_w2 = finish(sums)
    return output, grad_points, total_qkv, total_proj, total_w1, total_w2


def solution(mesh):
    placed = (P(AXES, None), P(AXES), P(AXES), P(AXES, None), P(), P(), P(), P())
    return jax.shard_map(
        on_device,
        mesh=mesh,
        in_specs=placed,
        out_specs=(P(AXES, None), P(AXES, None), P(), P(), P(), P()),
        check_vma=False,
    )
```

```python
import math

import jax
import jax.numpy as jnp
from jax import lax
from jax.experimental import pallas as pl
from jax.experimental.pallas import tpu as pltpu
from jax.sharding import PartitionSpec as P

AXES = ("blk", "sub")
ROWS = 1024
D = 384
FF = 1536
LANES = 128
HEAD_DIM = 32
GROUPS = D // LANES
HEADS_PER_GROUP = LANES // HEAD_DIM
SHARDS = 128
CAP = 32
SLOTS = SHARDS * CAP
STEP_SHARDS = 64
STEP_SLOTS = STEP_SHARDS * CAP
STEPS = SHARDS // STEP_SHARDS
WIRE_ROWS = 3 * CAP + 2
EPSILON = 1e-05
SCALING = 1.0 / math.sqrt(HEAD_DIM)
LOG2E = 1.4426950408889634
MASKED = -1e30
TILE = 256
BF = jnp.bfloat16
F32 = jnp.float32

NO_COST = pl.CostEstimate(flops=1, bytes_accessed=1, transcendentals=0)

NT = (((1,), (1,)), ((), ()))


def dot(a, b):
    return jnp.dot(a, b, preferred_element_type=F32)


def dot_nt(a, b):
    return lax.dot_general(a, b, NT, preferred_element_type=F32)


def iota(shape, axis):
    return lax.broadcasted_iota(jnp.int32, shape, axis)


def params(grid_dims=1, mib=56):
    return pltpu.CompilerParams(
        vmem_limit_bytes=mib * 1024 * 1024,
        dimension_semantics=("arbitrary",) * grid_dims,
    )


def row_to_column(row):
    return jnp.broadcast_to(row, (8, row.shape[1])).T[:, 0:1]


def one_hot_slots(slot_row, first):
    ids = iota((STEP_SLOTS, ROWS), 0) + first
    return (ids == slot_row).astype(F32).astype(BF)


def pack_points_kernel(lane_ref, pos_ref, x_ref, out_ref, slot_ref, high_s, low_s):
    step = pl.program_id(0)

    @pl.when(step == 0)
    def _():
        pos = pos_ref[...]
        target = pos >> 10
        offset = pos & (ROWS - 1)
        member = iota((SHARDS, ROWS), 0) == target
        member_bf = member.astype(F32).astype(BF)
        before = (iota((ROWS, ROWS), 0) < iota((ROWS, ROWS), 1)).astype(F32).astype(BF)
        earlier = dot(member_bf, before)
        rank = jnp.sum(jnp.where(member, earlier, 0.0), axis=0, keepdims=True).astype(jnp.int32)
        slot_ref[...] = target * CAP + rank
        lane = (iota((LANES, ROWS), 0) == rank + lane_ref[0]).astype(F32).astype(BF)
        high = ((offset >> 5) + 1).astype(F32)
        low = (offset & 31).astype(F32)
        high_s[...] = dot_nt(jnp.where(member, high, 0.0).astype(BF), lane)
        low_s[...] = dot_nt(jnp.where(member, low, 0.0).astype(BF), lane)

    picked = dot(one_hot_slots(slot_ref[...], step * STEP_SLOTS), x_ref[...]).astype(BF)
    for piece in range(3):
        out_ref[:, piece * CAP : (piece + 1) * CAP, :] = picked[
            :, piece * LANES : (piece + 1) * LANES
        ].reshape(STEP_SHARDS, CAP, LANES)
    first = pl.multiple_of(step * STEP_SHARDS, STEP_SHARDS)
    high = high_s[pl.ds(first, STEP_SHARDS), :]
    low = low_s[pl.ds(first, STEP_SHARDS), :]
    for s in range(STEP_SHARDS):
        pair = jnp.concatenate([high[s : s + 1], low[s : s + 1]], axis=0)
        out_ref[s, 3 * CAP : WIRE_ROWS, :] = pair.astype(BF)


def pack_points(first_lane, pos_row, points):
    return pl.pallas_call(
        pack_points_kernel,
        grid=(STEPS,),
        in_specs=[
            pl.BlockSpec(memory_space=pltpu.SMEM),
            pl.BlockSpec((1, ROWS), lambda i: (0, 0)),
            pl.BlockSpec((ROWS, D), lambda i: (0, 0)),
        ],
        out_specs=[
            pl.BlockSpec((STEP_SHARDS, WIRE_ROWS, LANES), lambda i: (i, 0, 0)),
            pl.BlockSpec((1, ROWS), lambda i: (0, 0)),
        ],
        out_shape=[
            jax.ShapeDtypeStruct((SHARDS, WIRE_ROWS, LANES), BF),
            jax.ShapeDtypeStruct((1, ROWS), jnp.int32),
        ],
        scratch_shapes=[pltpu.VMEM((SHARDS, LANES), F32), pltpu.VMEM((SHARDS, LANES), F32)],
        compiler_params=params(),
        cost_estimate=NO_COST,
        name="pack_points",
    )(first_lane, pos_row, points)


def pack_rows_kernel(slot_ref, x_ref, out_ref):
    picked = dot(one_hot_slots(slot_ref[...], pl.program_id(0) * STEP_SLOTS), x_ref[...])
    out_ref[...] = picked.astype(BF).reshape(STEP_SHARDS, CAP, D)


def pack_rows(slot_row, values):
    return pl.pallas_call(
        pack_rows_kernel,
        grid=(STEPS,),
        in_specs=[
            pl.BlockSpec((1, ROWS), lambda i: (0, 0)),
            pl.BlockSpec((ROWS, D), lambda i: (0, 0)),
        ],
        out_specs=pl.BlockSpec((STEP_SHARDS, CAP, D), lambda i: (i, 0, 0)),
        out_shape=jax.ShapeDtypeStruct((SHARDS, CAP, D), BF),
        compiler_params=params(),
        cost_estimate=NO_COST,
        name="pack_rows",
    )(slot_row, values)


def unpack_rows_kernel(slot_ref, home_ref, out_ref, column_s, total_s):
    step = pl.program_id(0)

    @pl.when(step == 0)
    def _():
        column_s[...] = jnp.broadcast_to(
            row_to_column(slot_ref[...].astype(F32)).astype(jnp.int32), (ROWS, LANES)
        )
        total_s[...] = jnp.zeros_like(total_s)

    wide = jnp.concatenate([column_s[...]] * (STEP_SLOTS // LANES), axis=1)
    hot = (iota((ROWS, STEP_SLOTS), 1) + step * STEP_SLOTS == wide).astype(F32).astype(BF)
    total_s[...] += dot(hot, home_ref[...].reshape(STEP_SLOTS, D))

    @pl.when(step == STEPS - 1)
    def _():
        out_ref[...] = total_s[...].astype(BF)


def unpack_rows(slot_row, home):
    return pl.pallas_call(
        unpack_rows_kernel,
        grid=(STEPS,),
        in_specs=[
            pl.BlockSpec((1, ROWS), lambda i: (0, 0)),
            pl.BlockSpec((STEP_SHARDS, CAP, D), lambda i: (i, 0, 0)),
        ],
        out_specs=pl.BlockSpec((ROWS, D), lambda i: (0, 0)),
        out_shape=jax.ShapeDtypeStruct((ROWS, D), BF),
        scratch_shapes=[pltpu.VMEM((ROWS, LANES), jnp.int32), pltpu.VMEM((ROWS, D), F32)],
        compiler_params=params(mib=36),
        cost_estimate=NO_COST,
        name="unpack_rows",
    )(slot_row, home)


def norm_parts(values):
    centred = values - jnp.mean(values, axis=-1, keepdims=True)
    spread = jnp.mean(centred * centred, axis=-1, keepdims=True)
    scale = lax.rsqrt(spread + EPSILON)
    return centred * scale, scale


def norm_pull(normed, scale, upstream):
    across = jnp.mean(upstream, axis=-1, keepdims=True)
    along = jnp.mean(upstream * normed, axis=-1, keepdims=True)
    return scale * (upstream - across - normed * along)


def landing_one_hot(landing):
    return (iota((ROWS, STEP_SLOTS), 0) == landing).astype(F32).astype(BF)


def land_points_kernel(recv_ref, w_ref, ordered_ref, packed_ref, landing_ref, total_s):
    step = pl.program_id(0)

    @pl.when(step == 0)
    def _():
        total_s[...] = jnp.zeros_like(total_s)

    pieces = []
    for group in range(STEP_SHARDS // 4):
        pair = recv_ref[4 * group, 3 * CAP : WIRE_ROWS, :].astype(F32)
        for other in range(1, 4):
            pair = pair + recv_ref[4 * group + other, 3 * CAP : WIRE_ROWS, :].astype(F32)
        pieces.append((pair[0:1] - 1.0) * 32.0 + pair[1:2])
    landing = jnp.concatenate(pieces, axis=1).astype(jnp.int32)
    landing_ref[0] = landing
    rows = jnp.concatenate(
        [
            recv_ref[:, piece * CAP : (piece + 1) * CAP, :].reshape(STEP_SLOTS, LANES)
            for piece in range(3)
        ],
        axis=1,
    )
    total_s[...] += dot(landing_one_hot(landing), rows)

    @pl.when(step == STEPS - 1)
    def _():
        ordered = total_s[...]
        ordered_ref[...] = ordered.astype(BF)
        normed, _ = norm_parts(ordered)
        packed_ref[...] = dot(normed.astype(BF), w_ref[...]).astype(BF)


def land_points(received, w_qkv):
    return pl.pallas_call(
        land_points_kernel,
        grid=(STEPS,),
        in_specs=[
            pl.BlockSpec((STEP_SHARDS, WIRE_ROWS, LANES), lambda i: (i, 0, 0)),
            pl.BlockSpec((D, 3 * D), lambda i: (0, 0)),
        ],
        out_specs=[
            pl.BlockSpec((ROWS, D), lambda i: (0, 0)),
            pl.BlockSpec((ROWS, 3 * D), lambda i: (0, 0)),
            pl.BlockSpec((1, 1, STEP_SLOTS), lambda i: (i, 0, 0)),
        ],
        out_shape=[
            jax.ShapeDtypeStruct((ROWS, D), BF),
            jax.ShapeDtypeStruct((ROWS, 3 * D), BF),
            jax.ShapeDtypeStruct((STEPS, 1, STEP_SLOTS), jnp.int32),
        ],
        scratch_shapes=[pltpu.VMEM((ROWS, D), F32)],
        compiler_params=params(),
        cost_estimate=NO_COST,
        name="land_points",
    )(received, w_qkv)


def land_rows_kernel(landing_ref, recv_ref, out_ref, total_s):
    step = pl.program_id(0)

    @pl.when(step == 0)
    def _():
        total_s[...] = jnp.zeros_like(total_s)

    total_s[...] += dot(landing_one_hot(landing_ref[0]), recv_ref[...].reshape(STEP_SLOTS, D))

    @pl.when(step == STEPS - 1)
    def _():
        out_ref[...] = total_s[...].astype(BF)


def land_rows(landing, received):
    return pl.pallas_call(
        land_rows_kernel,
        grid=(STEPS,),
        in_specs=[
            pl.BlockSpec((1, 1, STEP_SLOTS), lambda i: (i, 0, 0)),
            pl.BlockSpec((STEP_SHARDS, CAP, D), lambda i: (i, 0, 0)),
        ],
        out_specs=pl.BlockSpec((ROWS, D), lambda i: (0, 0)),
        out_shape=jax.ShapeDtypeStruct((ROWS, D), BF),
        scratch_shapes=[pltpu.VMEM((ROWS, D), F32)],
        compiler_params=params(),
        cost_estimate=NO_COST,
        name="land_rows",
    )(landing, received)


def return_one_hot(landing):
    column = row_to_column(landing.astype(F32)).astype(jnp.int32)
    return (iota((STEP_SLOTS, ROWS), 1) == column).astype(F32).astype(BF)


def return_rows_kernel(landing_ref, x_ref, out_ref):
    picked = dot(return_one_hot(landing_ref[0]), x_ref[...])
    out_ref[...] = picked.astype(BF).reshape(STEP_SHARDS, CAP, D)


def return_rows(landing, values):
    return pl.pallas_call(
        return_rows_kernel,
        grid=(STEPS,),
        in_specs=[
            pl.BlockSpec((1, 1, STEP_SLOTS), lambda i: (i, 0, 0)),
            pl.BlockSpec((ROWS, D), lambda i: (0, 0)),
        ],
        out_specs=pl.BlockSpec((STEP_SHARDS, CAP, D), lambda i: (i, 0, 0)),
        out_shape=jax.ShapeDtypeStruct((SHARDS, CAP, D), BF),
        compiler_params=params(),
        cost_estimate=NO_COST,
        name="return_rows",
    )(landing, values)


def three_parts(values):
    high = values.astype(BF)
    rest = values - high.astype(F32)
    middle = rest.astype(BF)
    return high, middle, (rest - middle.astype(F32)).astype(BF)


def write_bias(bias_s, column_ref, row_ref):
    bias_s[...] = jnp.where(column_ref[...] == row_ref[...], 0.0, MASKED)


def head_of_lane():
    return iota((ROWS, LANES), 1) // HEAD_DIM


def roll_lanes(values, by):
    return pltpu.roll(values.astype(F32), by % LANES, 1)


def query_side(q, head, owner, shift=None):
    near, far = (head + 1) % HEADS_PER_GROUP, (head + 2) % HEADS_PER_GROUP
    high, middle, low = (part.astype(F32) for part in three_parts(q * (SCALING * LOG2E)))
    side = jnp.where(
        owner == head,
        high,
        jnp.where(
            owner == near,
            roll_lanes(middle, HEAD_DIM),
            jnp.where(owner == far, roll_lanes(low, 2 * HEAD_DIM), 0.0),
        ),
    )
    if shift is not None:
        last = (head + 3) % HEADS_PER_GROUP
        lane = iota((ROWS, LANES), 1) - last * HEAD_DIM
        shift = roll_lanes(shift, 3 * HEAD_DIM)
        for at, part in enumerate(three_parts(-shift)):
            side = jnp.where(lane == at, part.astype(F32), side)
    return side.astype(BF)


def key_side(k, head, owner, shifted):
    near, far = (head + 1) % HEADS_PER_GROUP, (head + 2) % HEADS_PER_GROUP
    side = jnp.where(
        owner == head,
        k,
        jnp.where(
            owner == near,
            roll_lanes(k, HEAD_DIM),
            jnp.where(owner == far, roll_lanes(k, 2 * HEAD_DIM), 0.0),
        ),
    )
    if shifted:
        last = (head + 3) % HEADS_PER_GROUP
        lane = iota((ROWS, LANES), 1) - last * HEAD_DIM
        side = jnp.where((lane >= 0) & (lane < 3), 1.0, side)
    return side.astype(BF)


def attend_kernel(column_ref, row_ref, q_ref, k_ref, v_ref, mixed_ref, exact_ref, level_ref, bias_s):
    @pl.when(pl.program_id(0) == 0)
    def _():
        write_bias(bias_s, column_ref, row_ref)

    owner = head_of_lane()
    q, k, v = (ref[...].astype(F32) for ref in (q_ref, k_ref, v_ref))
    owner_tile = owner[:TILE]
    for head in range(HEADS_PER_GROUP):
        queries = query_side(q, head, owner)
        keys = key_side(k, head, owner, False)
        values = jnp.concatenate(
            [jnp.where(owner == head, v, 0.0).astype(BF), jnp.ones((ROWS, LANES), BF)], axis=1
        )
        for tile in range(ROWS // TILE):
            rows = slice(tile * TILE, (tile + 1) * TILE)
            scores = dot_nt(queries[rows], keys) + bias_s[rows, :]
            most = jnp.max(scores, axis=-1, keepdims=True)
            raised = jnp.exp2(scores - most).astype(BF)
            both = dot(raised, values)
            total = both[:, LANES:]
            result = both[:, :LANES] / total
            level = most + jnp.log2(total)
            if head == 0:
                exact_ref[rows, :] = result
                level_ref[rows, :] = level
            else:
                mine = owner_tile == head
                exact_ref[rows, :] = jnp.where(mine, result, exact_ref[rows, :])
                level_ref[rows, :] = jnp.where(mine, level, level_ref[rows, :])
    mixed_ref[...] = exact_ref[...].astype(BF)


def group_spec(first=0):
    return pl.BlockSpec((ROWS, LANES), lambda g: (0, first + g))


def whole(shape):
    return pl.BlockSpec(shape, lambda g: (0,) * len(shape))


def attend(segment_column, segment_row, packed):
    return pl.pallas_call(
        attend_kernel,
        grid=(GROUPS,),
        in_specs=[
            whole((ROWS, 1)),
            whole((1, ROWS)),
            group_spec(0),
            group_spec(GROUPS),
            group_spec(2 * GROUPS),
        ],
        out_specs=[group_spec()] * 3,
        out_shape=[
            jax.ShapeDtypeStruct((ROWS, D), BF),
            jax.ShapeDtypeStruct((ROWS, D), F32),
            jax.ShapeDtypeStruct((ROWS, D), F32),
        ],
        scratch_shapes=[pltpu.VMEM((ROWS, ROWS), F32)],
        compiler_params=params(),
        cost_estimate=NO_COST,
        name="attend",
    )(segment_column, segment_row, packed, packed, packed)


def attend_back_kernel(
    column_ref,
    row_ref,
    q_ref,
    k_ref,
    v_ref,
    up_ref,
    exact_ref,
    level_ref,
    out_ref,
    bias_s,
    dqt_s,
    dk_s,
    dv_s,
):
    @pl.when(pl.program_id(0) == 0)
    def _():
        write_bias(bias_s, column_ref, row_ref)

    owner = head_of_lane()
    q, k, v, up = (ref[...].astype(F32) for ref in (q_ref, k_ref, v_ref, up_ref))
    level = level_ref[...]
    keys_t = k.T.astype(BF)
    from_head = iota((LANES, LANES), 0) // HEAD_DIM
    to_head = iota((LANES, LANES), 1) // HEAD_DIM
    spread = ((from_head + 1) % HEADS_PER_GROUP == to_head).astype(F32).astype(BF)
    delta = sum(dot(part, spread) for part in three_parts(up * exact_ref[...]))
    delta_parts = [part.astype(F32) for part in three_parts(-delta)]
    for head in range(HEADS_PER_GROUP):
        mine = owner == head
        near = (head + 1) % HEADS_PER_GROUP
        lane = iota((ROWS, LANES), 1) - near * HEAD_DIM
        queries = query_side(q, head, owner, level)
        keys = key_side(k, head, owner, True)
        up_mine = jnp.where(mine, up, 0.0)
        up_side = up_mine
        for at, part in enumerate(delta_parts):
            up_side = jnp.where(lane == at, part, up_side)
        up_side = up_side.astype(BF)
        up_mine = up_mine.astype(BF)
        value_side = jnp.where((lane >= 0) & (lane < 3), 1.0, v).astype(BF)
        query_mine = jnp.where(mine, q, 0.0).astype(BF)
        head_rows = slice(head * HEAD_DIM, (head + 1) * HEAD_DIM)
        dv_part = dk_part = 0.0
        for tile in range(ROWS // TILE):
            at = slice(tile * TILE, (tile + 1) * TILE)
            weights = jnp.exp2(dot_nt(keys, queries[at]) + bias_s[:, at])
            pulled = (weights * dot_nt(value_side, up_side[at])).astype(BF)
            dv_part = dv_part + dot(weights.astype(BF), up_mine[at])
            dk_part = dk_part + dot(pulled, query_mine[at])
            dqt_s[head_rows, at] = dot(keys_t[head_rows], pulled)
        if head == 0:
            dv_s[...] = dv_part
            dk_s[...] = dk_part
        else:
            dv_s[...] += dv_part
            dk_s[...] += dk_part
    out_ref[:, :LANES] = (dqt_s[...] * SCALING).T.astype(BF)
    out_ref[:, LANES : 2 * LANES] = (dk_s[...] * SCALING).astype(BF)
    out_ref[:, 2 * LANES :] = dv_s[...].astype(BF)


def attend_back(segment_column, segment_row, packed, upstream, exact, level):
    return pl.pallas_call(
        attend_back_kernel,
        grid=(GROUPS,),
        in_specs=[
            whole((ROWS, 1)),
            whole((1, ROWS)),
            group_spec(0),
            group_spec(GROUPS),
            group_spec(2 * GROUPS),
            group_spec(),
            group_spec(),
            group_spec(),
        ],
        out_specs=pl.BlockSpec((ROWS, 3 * LANES), lambda g: (0, g)),
        out_shape=jax.ShapeDtypeStruct((ROWS, 3 * D), BF),
        scratch_shapes=[
            pltpu.VMEM((ROWS, ROWS), F32),
            pltpu.VMEM((LANES, ROWS), F32),
            pltpu.VMEM((ROWS, LANES), F32),
            pltpu.VMEM((ROWS, LANES), F32),
        ],
        compiler_params=params(),
        cost_estimate=NO_COST,
        name="attend_back",
    )(segment_column, segment_row, packed, packed, packed, upstream, exact, level)


FORWARD_STEP = 512
BACK_STEP = 512


def mlp_kernel(
    ordered_ref,
    mixed_ref,
    w_proj_ref,
    w1_ref,
    w2_ref,
    block_ref,
    middle_ref,
    hidden_ref,
    slope_ref,
    normed_s,
    out_s,
):
    step = pl.program_id(0)

    @pl.when(step == 0)
    def _():
        middle = (
            ordered_ref[...].astype(F32) + dot(mixed_ref[...], w_proj_ref[...])
        ).astype(BF)
        middle_ref[...] = middle
        normed, _ = norm_parts(middle.astype(F32))
        normed_s[...] = normed.astype(BF)
        out_s[...] = middle.astype(F32)

    before = dot(normed_s[...], w1_ref[...])
    half = 0.5 * (1.0 + lax.erf(before * math.sqrt(0.5)))
    density = jnp.exp(before * before * -0.5) * (1.0 / math.sqrt(2.0 * math.pi))
    hidden = (before * half).astype(BF)
    hidden_ref[...] = hidden
    slope_ref[...] = half + before * density
    out_s[...] += dot(hidden, w2_ref[...])

    @pl.when(step == FF // FORWARD_STEP - 1)
    def _():
        block_ref[...] = out_s[...].astype(BF)


def mlp(ordered, mixed, w_proj, w_fc1, w_fc2):
    rows = whole((ROWS, D))
    wide = pl.BlockSpec((ROWS, FORWARD_STEP), lambda i: (0, i))
    return pl.pallas_call(
        mlp_kernel,
        grid=(FF // FORWARD_STEP,),
        in_specs=[
            rows,
            rows,
            whole((D, D)),
            pl.BlockSpec((D, FORWARD_STEP), lambda i: (0, i)),
            pl.BlockSpec((FORWARD_STEP, D), lambda i: (i, 0)),
        ],
        out_specs=[rows, rows, wide, wide],
        out_shape=[
            jax.ShapeDtypeStruct((ROWS, D), BF),
            jax.ShapeDtypeStruct((ROWS, D), BF),
            jax.ShapeDtypeStruct((ROWS, FF), BF),
            jax.ShapeDtypeStruct((ROWS, FF), F32),
        ],
        scratch_shapes=[pltpu.VMEM((ROWS, D), BF), pltpu.VMEM((ROWS, D), F32)],
        compiler_params=params(),
        cost_estimate=NO_COST,
        name="mlp",
    )(ordered, mixed, w_proj, w_fc1, w_fc2)


def mlp_back_kernel(
    up_ref,
    middle_ref,
    slope_ref,
    w_proj_ref,
    w1_ref,
    w2_ref,
    d_middle_ref,
    d_mixed_ref,
    d_before_ref,
    d_normed_s,
):
    step = pl.program_id(0)
    up = up_ref[...]
    d_hidden = dot_nt(up, w2_ref[...]).astype(BF).astype(F32)
    d_before = (d_hidden * slope_ref[...]).astype(BF)
    d_before_ref[...] = d_before
    part = dot_nt(d_before, w1_ref[...])

    @pl.when(step == 0)
    def _():
        d_normed_s[...] = part

    @pl.when(step > 0)
    def _():
        d_normed_s[...] += part

    @pl.when(step == FF // BACK_STEP - 1)
    def _():
        normed, scale = norm_parts(middle_ref[...].astype(F32))
        pulled = norm_pull(normed, scale, d_normed_s[...].astype(BF).astype(F32)).astype(BF)
        d_middle = (up.astype(F32) + pulled.astype(F32)).astype(BF)
        d_middle_ref[...] = d_middle
        d_mixed_ref[...] = dot_nt(d_middle, w_proj_ref[...]).astype(BF)


def mlp_back(upstream, middle, slope, w_proj, w_fc1, w_fc2):
    rows = whole((ROWS, D))
    wide = pl.BlockSpec((ROWS, BACK_STEP), lambda i: (0, i))
    return pl.pallas_call(
        mlp_back_kernel,
        grid=(FF // BACK_STEP,),
        in_specs=[
            rows,
            rows,
            wide,
            whole((D, D)),
            pl.BlockSpec((D, BACK_STEP), lambda i: (0, i)),
            pl.BlockSpec((BACK_STEP, D), lambda i: (i, 0)),
        ],
        out_specs=[rows, rows, wide],
        out_shape=[
            jax.ShapeDtypeStruct((ROWS, D), BF),
            jax.ShapeDtypeStruct((ROWS, D), BF),
            jax.ShapeDtypeStruct((ROWS, FF), BF),
        ],
        scratch_shapes=[pltpu.VMEM((ROWS, D), F32)],
        compiler_params=params(),
        cost_estimate=NO_COST,
        name="mlp_back",
    )(upstream, middle, slope, w_proj, w_fc1, w_fc2)


def group_columns(part, group):
    first = part * D + group * LANES
    return slice(first, first + LANES)


def inputs_back_kernel(
    landing_ref, ordered_ref, d_packed_ref, d_middle_ref, w_ref, out_ref, d_inputs_s
):
    @pl.when(pl.program_id(0) == 0)
    def _():
        normed, scale = norm_parts(ordered_ref[...].astype(F32))
        weights = jnp.concatenate(
            [
                w_ref[:, group_columns(part, group)]
                for group in range(GROUPS)
                for part in range(3)
            ],
            axis=1,
        )
        d_normed = dot_nt(d_packed_ref[...], weights)
        pulled = norm_pull(normed, scale, d_normed.astype(BF).astype(F32)).astype(BF)
        d_inputs_s[...] = (d_middle_ref[...].astype(F32) + pulled.astype(F32)).astype(BF)

    picked = dot(return_one_hot(landing_ref[0]), d_inputs_s[...])
    out_ref[...] = picked.astype(BF).reshape(STEP_SHARDS, CAP, D)


def inputs_back(landing, ordered, d_packed, d_middle, w_qkv):
    rows = whole((ROWS, D))
    return pl.pallas_call(
        inputs_back_kernel,
        grid=(STEPS,),
        in_specs=[
            pl.BlockSpec((1, 1, STEP_SLOTS), lambda i: (i, 0, 0)),
            rows,
            whole((ROWS, 3 * D)),
            rows,
            whole((D, 3 * D)),
        ],
        out_specs=pl.BlockSpec((STEP_SHARDS, CAP, D), lambda i: (i, 0, 0)),
        out_shape=jax.ShapeDtypeStruct((SHARDS, CAP, D), BF),
        scratch_shapes=[pltpu.VMEM((ROWS, D), BF)],
        compiler_params=params(),
        cost_estimate=NO_COST,
        name="inputs_back",
    )(landing, ordered, d_packed, d_middle, w_qkv)


def transposed(values):
    return values.astype(F32).T.astype(BF)


def weights_back_kernel(
    ordered_ref,
    middle_ref,
    mixed_ref,
    d_middle_ref,
    up_ref,
    d_packed_ref,
    d_before_ref,
    hidden_ref,
    d_w1_ref,
    d_w2_ref,
    rest_ref,
    normed_t_s,
    again_t_s,
    up_t_s,
):
    step = pl.program_id(0)

    @pl.when(step == 0)
    def _():
        normed_t_s[...] = transposed(norm_parts(ordered_ref[...].astype(F32))[0].astype(BF))
        again_t_s[...] = transposed(norm_parts(middle_ref[...].astype(F32))[0].astype(BF))
        up_t_s[...] = transposed(up_ref[...])

    d_w1_ref[...] = dot(again_t_s[...], d_before_ref[...]).astype(BF)
    d_w2_ref[...] = dot(up_t_s[...], hidden_ref[...]).T.astype(BF)

    @pl.when(step < GROUPS)
    def _():
        rest_ref[...] = dot(normed_t_s[...], d_packed_ref[...]).astype(BF)

    @pl.when(step == GROUPS)
    def _():
        rest_ref[...] = dot(transposed(mixed_ref[...]), d_middle_ref[...]).astype(BF)


def weights_back(ordered, middle, mixed, d_middle, upstream, d_packed, d_before, hidden):
    rows = whole((ROWS, D))
    wide = pl.BlockSpec((ROWS, D), lambda i: (0, i))
    down = pl.BlockSpec((D, D), lambda i: (i, 0))
    return pl.pallas_call(
        weights_back_kernel,
        grid=(FF // D,),
        in_specs=[rows] * 5
        + [pl.BlockSpec((ROWS, D), lambda i: (0, jnp.minimum(i, GROUPS - 1))), wide, wide],
        out_specs=[down] * 3,
        out_shape=[jax.ShapeDtypeStruct((FF, D), BF)] * 3,
        scratch_shapes=[pltpu.VMEM((D, ROWS), BF)] * 3,
        compiler_params=params(mib=36),
        cost_estimate=NO_COST,
        name="weights_back",
    )(ordered, middle, mixed, d_middle, upstream, d_packed, d_before, hidden)


def place(axis):
    name, stride, size = {
        "y": ("blk", 2, 4),
        "core": ("blk", 1, 2),
        "x": ("sub", 4, 4),
        "z": ("sub", 1, 4),
    }[axis]
    return name, stride, size


def swap(values, axis, kind):
    name, stride, size = place(axis)
    pairs = []
    for index in range(lax.axis_size(name)):
        c = index // stride % size
        partner = 3 - c if kind else c ^ 1
        pairs.append((index, index + (partner - c) * stride))
    return lax.ppermute(values, name, pairs)


def side(axis, kind):
    name, stride, size = place(axis)
    c = lax.axis_index(name) // stride % size
    return c >> 1 if kind else (c ^ (c >> 1)) & 1


def add(a, b):
    return (a.astype(F32) + b.astype(F32)).astype(BF)


def halve_begin(values, axis, kind):
    keep = side(axis, kind)
    half = values.shape[0] // 2
    own = lax.dynamic_slice_in_dim(values, keep * half, half, 0)
    away = lax.dynamic_slice_in_dim(values, (1 - keep) * half, half, 0)
    return own, swap(away, axis, kind)


def halve(values, axis, kind):
    return add(*halve_begin(values, axis, kind))


def meet_begin(values, axis, kind):
    return values, swap(values, axis, kind)


def meet(values, axis, kind):
    return add(*meet_begin(values, axis, kind))


def double(values, axis, kind):
    other = swap(values, axis, kind)
    first = side(axis, kind) == 0
    return jnp.where(
        first, jnp.concatenate([values, other]), jnp.concatenate([other, values])
    )


def spread_again(values, axis):
    for kind in (1, 0):
        values = double(values, axis, kind)
    return values


def finish_kernel(
    keep_ref, w1_ref, w1_other_ref, w2_ref, w2_other_ref, rest_ref, rest_other_ref, qkv_ref, proj_ref, out1_ref, out2_ref
):
    step = pl.program_id(0)
    own = step // 2 == keep_ref[0]

    def block(mine_ref, other_ref):
        return jnp.where(own, mine_ref[...].astype(F32), other_ref[...].astype(F32))

    out1_ref[...] = block(w1_ref, w1_other_ref)
    out2_ref[...] = block(w2_ref, w2_other_ref)
    rest = block(rest_ref, rest_other_ref)
    for group in range(GROUPS):

        @pl.when(step == group)
        def _(group=group):
            for part in range(3):
                qkv_ref[:, group_columns(part, group)] = rest[:, part * LANES : (part + 1) * LANES]

    @pl.when(step == GROUPS)
    def _():
        proj_ref[...] = rest


def finish(sums):
    keep = side("core", 0).astype(jnp.int32).reshape(1)
    halves = [part for mine in sums for part in (mine, swap(mine, "core", 0))]
    half = pl.BlockSpec((D, D), lambda i: (i % 2, 0))
    return pl.pallas_call(
        finish_kernel,
        grid=(FF // D,),
        in_specs=[pl.BlockSpec(memory_space=pltpu.SMEM)] + [half] * 6,
        out_specs=[
            whole((D, 3 * D)),
            whole((D, D)),
            pl.BlockSpec((D, D), lambda i: (0, i)),
            pl.BlockSpec((D, D), lambda i: (i, 0)),
        ],
        out_shape=[
            jax.ShapeDtypeStruct((D, 3 * D), F32),
            jax.ShapeDtypeStruct((D, D), F32),
            jax.ShapeDtypeStruct((D, FF), F32),
            jax.ShapeDtypeStruct((FF, D), F32),
        ],
        compiler_params=params(mib=36),
        cost_estimate=NO_COST,
        name="finish",
    )(keep, *halves)


together = lax.optimization_barrier


def exchange(values):
    return lax.all_to_all(values, AXES, split_axis=0, concat_axis=0, tiled=True)


def on_device(points, hilbert_pos, segment_ids, cotangent, w_qkv, w_proj, w_fc1, w_fc2):
    first_lane = ((lax.axis_index(AXES) % 4) * CAP).astype(jnp.int32).reshape(1)
    segment_row = segment_ids.reshape(1, ROWS)
    segment_column = segment_ids.reshape(ROWS, 1)
    wire, slot_row = pack_points(first_lane, hilbert_pos.reshape(1, ROWS), points)
    ordered, packed, landing = land_points(exchange(wire), w_qkv)
    up_slots, segment_column = together((pack_rows(slot_row, cotangent), segment_column))
    up_received = exchange(up_slots)
    mixed, exact, level = attend(segment_column, segment_row, packed)
    block, middle, hidden, slope = mlp(ordered, mixed, w_proj, w_fc1, w_fc2)
    returned, up_received = together((return_rows(landing, block), up_received))
    output_home = exchange(returned)
    upstream = land_rows(landing, up_received)
    d_middle, d_mixed, d_before = mlp_back(upstream, middle, slope, w_proj, w_fc1, w_fc2)
    d_packed = attend_back(segment_column, segment_row, packed, d_mixed, exact, level)
    d_packed, output_home = together((d_packed, output_home))
    back = inputs_back(landing, ordered, d_packed, d_middle, w_qkv)
    grad_home = exchange(back)
    d_packed, output_home, _ = together((d_packed, output_home, back))
    sums = weights_back(ordered, middle, mixed, d_middle, upstream, d_packed, d_before, hidden)
    sums = [halve_begin(part, "core", 0) for part in sums]
    output = unpack_rows(slot_row, output_home)
    sums, output, grad_home = together((sums, output, grad_home))
    orders = (("y", "x", "z"), ("x", "z", "y"), ("z", "y", "x"))
    sums = [halve_begin(add(*part), order[0], 0) for part, order in zip(sums, orders)]
    grad_points = unpack_rows(slot_row, grad_home)
    sums, grad_points = together((sums, grad_points))
    sums = [halve(add(*part), order[0], 1) for part, order in zip(sums, orders)]
    for place_in_order in (1, 2):
        for kind in (0, 1):
            sums = [meet(part, order[place_in_order], kind) for part, order in zip(sums, orders)]
    sums = [spread_again(part, order[0]) for part, order in zip(sums, orders)]
    total_qkv, total_proj, total_w1, total_w2 = finish(sums)
    return output, grad_points, total_qkv, total_proj, total_w1, total_w2


def solution(mesh):
    placed = (P(AXES, None), P(AXES), P(AXES), P(AXES, None), P(), P(), P(), P())
    return jax.shard_map(
        on_device,
        mesh=mesh,
        in_specs=placed,
        out_specs=(P(AXES, None), P(AXES, None), P(), P(), P(), P()),
        check_vma=False,
    )
```
